512 devices in a mesh: tm: 32 (over z, y_lo), space: 16 (over x, y_hi, core).
Axes of the slice: x: 4, y: 4 (y_hi: 2, y_lo: 2; y = y_hi * 2 + y_lo), z: 16, core: 2. Of those that a mesh axis runs over, the one named last changes fastest.
Arguments:
- inner_x: bfloat16 [32, 64, 64, 1536], P('tm', 'space'), may hold values from -6 to 6
- inner_z: bfloat16 [32, 64, 64, 1536], P('tm', 'space'), may hold values from -6 to 6
- conv_weight: float32 [4, 1536], P(None, 'space'), may hold values from -3 to 3
- conv_bias: float32 [1536], P('space'), may hold values from -0.5 to 0.5
- proj_weight: bfloat16 [1536, 80], P('space'), may hold values from -0.15625 to 0.15625
- step_weight: bfloat16 [48, 1536], P(None, 'space'), may hold values from -0.875 to 0.875
- step_bias: float32 [1536], P('space'), may hold values from -6.91 to -2.25, as said below
- decay_log: float32 [16, 1536], P(None, 'space'), may hold values from -2 to 2.77
- skip_gain: float32 [1536], P('space'), may hold values from 0.5 to 1.5
- out_weight: bfloat16 [1536, 768], replicated, may hold values from -0.15625 to 0.15625
- order_table: int32 [32], replicated, may hold values from 0 to 31, each once
Outputs:
- mixed: bfloat16 [32, 64, 64, 768], P('tm', 'space')
The draws below stay inside these ranges and needn't reach their ends.
Inputs may be any that keep to these rules, and one draw needn't show every extreme that they name: order_table names each of the 32 blocks of a frame exactly once. step_bias is the inverse softplus of step sizes between 0.001 and 0.1.
All inputs are finite; a program needn't handle non-finite values.
Results may differ from the reference program's by a relative error of at most 0.017.
Values may be sent and summed in bfloat16 or wider, within the bound.
A program may use at most 128 MiB of HBM per device.

```python
import jax
import jax.numpy as jnp
from jax import lax

D = 768
DI = 1536
NS = 16
DTR = 48
KC = 4
H = 64
W = 64
BLK = 128
FRAMES = 32
NBF = 32


def draw_step_bias(key, part):
    key = jax.random.fold_in(key, 11)
    unit = jax.random.uniform(key, (DI,), jnp.float32)
    step = 0.001 * jnp.exp(unit * jnp.log(100.0))
    return jnp.log(jnp.expm1(step))


def level_of(stream_key, shape, pieces, low, largest):
    level, own = 1.0, jax.random.fold_in(stream_key, 6)
    for dim, shards_of in pieces:
        heights = jnp.exp(jax.random.uniform(jax.random.fold_in(own, dim), (shards_of,), jnp.float32, low / len(pieces), largest / len(pieces)))
        level = level * jnp.repeat(heights, shape[dim] // shards_of).reshape([-1 if axis == dim else 1 for axis in range(len(shape))])
    return level


def bell_draw(stream_key, extent, deviation, bound, shards=(), held_as=jnp.bfloat16):
    entries = jax.random.normal(stream_key, extent, jnp.float32) * deviation
    if len(shards) > 0:
        entries = level_of(stream_key, extent, shards, -0.22, 0.18) * entries
    return jnp.clip(entries, min=-bound, max=bound).astype(held_as)


def setup_inputs(seed: int = 0) -> dict:
    streams_of = jax.random.split(jax.random.key(seed), 12)
    inner_x = bell_draw(streams_of[0], (FRAMES, H, W, DI), 1.0, 6.0, ((0, 32), (1, 16)))
    inner_z = bell_draw(streams_of[1], (FRAMES, H, W, DI), 1.0, 6.0, ((0, 32), (1, 16)))
    conv_weight = bell_draw(streams_of[2], (KC, DI), KC ** -0.5, 3.0, ((1, 16),), jnp.float32)
    conv_bias = jnp.clip(jax.random.uniform(streams_of[3], (DI,), jnp.float32, -0.5, 0.5) * level_of(streams_of[3], (DI,), ((0, 16),), -0.4, 0.0), -0.5, 0.5)
    proj_weight = bell_draw(streams_of[4], (DI, DTR + 2 * NS), DI ** -0.5, 0.15625, ((0, 16),))
    step_weight = bell_draw(streams_of[5], (DTR, DI), DTR ** -0.5, 0.875, ((1, 16),))
    step_bias = draw_step_bias(jax.random.fold_in(streams_of[11], 71), 0)
    decay_log = jnp.clip(-2.0 + 4.77 * jax.random.uniform(streams_of[7], (NS, DI), jnp.float32) ** level_of(streams_of[7], (NS, DI), ((1, 16),), -0.2, 0.2), -2.0, 2.77)
    skip_gain = jnp.clip(0.5 + 1.0 * jax.random.uniform(streams_of[8], (DI,), jnp.float32) ** level_of(streams_of[8], (DI,), ((0, 16),), -0.2, 0.2), 0.5, 1.5)
    out_weight = bell_draw(streams_of[9], (DI, D), DI ** -0.5, 0.15625)
    order_table = jax.random.permutation(streams_of[10], NBF).astype(jnp.int32)
    return dict(inner_x=inner_x, inner_z=inner_z, conv_weight=conv_weight, conv_bias=conv_bias, proj_weight=proj_weight, step_weight=step_weight, step_bias=step_bias, decay_log=decay_log, skip_gain=skip_gain, out_weight=out_weight, order_table=order_table)


def reference(inner_x, inner_z, conv_weight, conv_bias, proj_weight, step_weight, step_bias, decay_log, skip_gain, out_weight, order_table):
    frames = inner_x.shape[0]
    frame_len = H * W
    ordered = inner_x.reshape(frames, frame_len // BLK, BLK, DI)[:, order_table].reshape(frames, frame_len, DI)
    rate = -jnp.exp(decay_log)

    def token_step(state, inputs):
        step_now, driving, in_now, out_now = inputs
        state = jnp.exp(step_now[None, :] * rate) * state + in_now[:, None] * driving[None, :]
        return state, jnp.sum(out_now[:, None] * state, axis=0)

    def frame_step(frame_state, frame_x):
        tail_rows, state = frame_state
        padded = jnp.concatenate([tail_rows, frame_x], axis=0).astype(jnp.float32)
        filtered = conv_bias[None, :] + sum(conv_weight[tap][None, :] * padded[tap:tap + frame_len] for tap in range(KC))
        signal = jax.nn.silu(filtered).astype(jnp.bfloat16)
        projected = jnp.dot(signal, proj_weight, preferred_element_type=jnp.float32)
        step_size = jax.nn.softplus(jnp.dot(projected[:, :DTR], step_weight.astype(jnp.float32), precision=lax.Precision.HIGHEST) + step_bias[None, :])
        in_coeff = projected[:, DTR:DTR + NS]
        out_coeff = projected[:, DTR + NS:]
        signal_f = signal.astype(jnp.float32)
        state, results = lax.scan(token_step, state, (step_size, step_size * signal_f, in_coeff, out_coeff))
        scanned = (results + skip_gain[None, :] * signal_f).astype(jnp.bfloat16)
        return (frame_x[frame_len - (KC - 1):], state), scanned

    initial = (jnp.zeros((KC - 1, DI), inner_x.dtype), jnp.zeros((NS, DI), jnp.float32))
    unused, scanned = lax.scan(frame_step, initial, ordered)
    blocks = scanned.reshape(frames, frame_len // BLK, BLK, DI)
    placed = jnp.zeros_like(blocks).at[:, order_table].set(blocks).reshape(frames * frame_len, DI)
    gate_rows = inner_z.reshape(frames * frame_len, DI).astype(jnp.float32)
    gated = (placed.astype(jnp.float32) * jax.nn.silu(gate_rows)).astype(jnp.bfloat16)
    output = jnp.dot(gated, out_weight, preferred_element_type=jnp.float32).astype(jnp.bfloat16)
    return output.reshape(frames, H, W, D)
```

```python
import jax
import jax.numpy as jnp
from jax import lax
from jax.experimental import pallas as pl
from jax.experimental.pallas import tpu as pltpu
from jax.sharding import PartitionSpec as P

MESH = pl.DeviceIdType.MESH
NS = 16
DTR = 48
KC = 4
BLK = 128
NBF = 32
DI = 1536
D = 768
TOK = 256
CH = 96
LANES = 128
TILES = DI // LANES
CHUNKS = 8
STEPS = TOK // CHUNKS
WROWS = 24
TROWS = 48
WB = DTR + DTR + 2 * NS
SEATS = 8
VMEM_LIMIT = 56 * 1024 * 1024
LOG2E = 1.4426950408889634
F32 = jnp.float32
BF16 = jnp.bfloat16


def scan_rows():
    r = lax.broadcasted_iota(jnp.int32, (TOK, TOK), 0)
    i = lax.broadcasted_iota(jnp.int32, (TOK, TOK), 1)
    return ((r % CHUNKS) * STEPS + r // CHUNKS == i).astype(F32).astype(BF16)


def token_rows():
    i = lax.broadcasted_iota(jnp.int32, (TOK, TOK), 0)
    r = lax.broadcasted_iota(jnp.int32, (TOK, TOK), 1)
    return ((r % CHUNKS) * STEPS + r // CHUNKS == i).astype(F32).astype(BF16)


def silu(v):
    half = 0.5 * v
    return half + half * jnp.tanh(half)


def lanes_of(tile, width=LANES):
    return pl.ds(pl.multiple_of(tile * width, width), width)


def spread_columns(projected, first, out):
    for n in range(NS):
        out[n] = jnp.broadcast_to(projected[:, first + n : first + n + 1], (TOK, LANES))


def layer(
    x, z, cw, cb, pwt, sw, sb, dl, sg, ow, order, out,
    xv, zv, owv, gwf, gwb, gt, tstage, tsend, trecv, where_to,
    wfa, wba, xf, sigt, gz, signal, step, rate2, rate_own, in_b, out_b, inner, reach, y, gated, grown,
    sends, recv, scan_e, scan_p, pk1, got1, pk2, got2, bsend, back,
    local, s1, r1, s2, r2, st, rt, sa, ra, sb1, rb1, sc, rc, sd, rd,
):
    f = lax.axis_index("tm")
    s = lax.axis_index("space")
    frames = lax.axis_size("tm")
    width = lax.axis_size("space")
    outer = frames // SEATS
    row = s // 4
    side = s // 2 % 2
    core = s % 2
    part = f // SEATS
    seat = f % SEATS
    sibling = (f, s - core + 1 - core)
    ahead = ((f + 1) % frames, s)
    behind = ((f + frames - 1) % frames, s)
    full = (CHUNKS, LANES)
    slot = (3, CHUNKS, LANES)
    sub = lax.broadcasted_iota(jnp.int32, full, 0)
    sub3 = lax.broadcasted_iota(jnp.int32, slot, 1)
    zero = jnp.zeros(full, F32)

    def near(d):
        return part * SEATS + (seat + d) % SEATS

    def far(d):
        return ((part + d) % outer) * SEATS + seat

    def remote(src, dst, ssem, rsem, target):
        return pltpu.make_async_remote_copy(
            src_ref=src,
            dst_ref=dst,
            send_sem=ssem,
            recv_sem=rsem,
            device_id=target,
            device_id_type=MESH,
        )

    def push(src, dst, ssem, rsem, target):
        copy = remote(src, dst, ssem, rsem, target)
        copy.start()
        return copy

    load_x = pltpu.make_async_copy(x, xv, local.at[0])
    load_z = pltpu.make_async_copy(z, zv, local.at[1])
    load_ow = pltpu.make_async_copy(ow, owv, local.at[2])
    load_x.start()

    barrier = pltpu.get_barrier_semaphore()
    for d in range(1, width):
        pl.semaphore_signal(barrier, inc=1, device_id=(f, (s + d) % width), device_id_type=MESH)
    for d in range(1, SEATS):
        pl.semaphore_signal(barrier, inc=1, device_id=(near(d), s), device_id_type=MESH)
    for d in range(1, outer):
        pl.semaphore_signal(barrier, inc=1, device_id=(far(d), s), device_id_type=MESH)
    pl.semaphore_signal(barrier, inc=1, device_id=behind, device_id_type=MESH)

    load_z.start()
    load_ow.start()
    gwf[s, 0:KC] = cw[...]
    gwf[s, KC : KC + 1] = cb[...]
    gwf[s, 5:6] = sb[...]
    gwf[s, 6:7] = sg[...]
    gwf[s, 7:8] = jnp.zeros((1, CH), F32)
    gwf[s, 8:WROWS] = dl[...]
    gwb[s, 0:DTR] = sw[...]
    gwb[s, DTR:WB] = pwt[...]
    tstage[...] = jnp.zeros_like(tstage)
    load_x.wait()
    for b in range(2):
        ends = xv[BLK * (b + 1) - 16 : BLK * (b + 1)].astype(F32)
        for t in range(KC - 1):
            for j in range(TILES):
                line = ends[13 + t : 14 + t, LANES * j : LANES * (j + 1)]
                tstage[b, t * TILES + j : t * TILES + j + 1] = line
    gt[pl.ds(2 * s, 2)] = tstage[...].astype(BF16)
    pl.semaphore_wait(barrier, width + SEATS + outer - 2)

    def chip(dx, dy):
        return (row + dx) % 4 * 4 + (side + dy) % 2 * 2 + core

    def place(a, i):
        return (gwf.at[i], gt.at[pl.ds(2 * i, 2)], gwb.at[i])[a]

    sent = []
    relayed = [0, 0, 0]

    def relay(a, dx, dy, tx, ty):
        ref = place(a, chip(dx, dy))
        landing = (dx - tx) % 4 * 2 + (dy - ty) % 2
        ssem = s1.at[a, relayed[a]]
        relayed[a] += 1
        sent.append(push(ref, ref, ssem, r1.at[a, landing], (f, chip(tx, ty))))

    def share(a, dx, dy):
        ref = place(a, chip(dx, dy))
        k = dx * 2 + dy
        sent.append(push(ref, ref, s2.at[a, k], r2.at[a, k], sibling))

    def take(a, dx, dy):
        ref = place(a, chip(dx, dy))
        remote(ref, ref, s1.at[a, 0], r1.at[a, dx * 2 + dy], sibling).wait_recv()

    def own_item(a):
        relay(a, 0, 0, 1, 0)
        relay(a, 0, 0, 3, 0)
        relay(a, 0, 0, 0, 1)
        share(a, 0, 0)

    def other_side(a):
        take(a, 0, 1)
        relay(a, 0, 1, 1, 0)
        relay(a, 0, 1, 3, 0)
        share(a, 0, 1)

    def neighbours(a):
        came, onward = ((1, 3), (1, 3), (3, 1))[a]
        for dy in range(2):
            take(a, came, dy)
            relay(a, came, dy, onward, 0)
            share(a, came, dy)
        for dy in range(2):
            take(a, onward, dy)
            share(a, onward, dy)

    def opposite(a):
        for dy in range(2):
            take(a, 2, dy)
            share(a, 2, dy)

    def from_sibling(a):
        for dx in range(4):
            for dy in range(2):
                ref = place(a, chip(dx, dy) - core + 1 - core)
                k = dx * 2 + dy
                remote(ref, ref, s2.at[a, k], r2.at[a, k], sibling).wait_recv()

    for a in range(3):
        own_item(a)
    listed = [order[j] for j in range(NBF)]

    def inverse(r, carry):
        found = 0
        for j in range(NBF):
            found = jnp.where(listed[j] == r, j, found)
        where_to[r] = found
        return carry

    lax.fori_loop(0, NBF, inverse, 0)
    for b in range(2):
        xf[b, 0:8] = jnp.zeros((8, DI), F32)

    def widen(tile, carry):
        lanes = lanes_of(tile)
        for b in range(2):
            xf[b, 8 : 8 + BLK, lanes] = xv[BLK * b : BLK * (b + 1), lanes].astype(F32)
        return carry

    lax.fori_loop(0, TILES, widen, 0)
    sends[...] = jnp.zeros_like(sends)
    other_side(0)
    other_side(1)
    neighbours(0)
    opposite(0)
    neighbours(1)
    other_side(2)
    from_sibling(0)
    for i in range(DI // CH):
        wfa[:, CH * i : CH * (i + 1)] = gwf[i]

    def filtered(b, count, lanes):
        total = wfa[4:5, lanes]
        for k in range(KC):
            total = total + wfa[k : k + 1, lanes] * xf[b, 5 + k : 5 + k + count, lanes]
        return silu(total).astype(BF16)

    def convolve(tile, carry):
        lanes = lanes_of(tile)
        for b in range(2):
            sigt[BLK * b : BLK * (b + 1), lanes] = filtered(b, BLK, lanes)
        return carry

    lax.fori_loop(0, 3, convolve, 0)
    opposite(1)
    neighbours(2)
    lax.fori_loop(3, 6, convolve, 0)
    from_sibling(1)
    tsend[...] = gt[order[NBF - 1]]
    sent_tail = push(tsend, trecv, st, rt, ahead)
    sent.append(sent_tail)
    opposite(2)
    lax.fori_loop(6, TILES, convolve, 0)
    rate2[...] = -jnp.exp(wfa[8:WROWS]) * LOG2E
    rearranged = scan_rows()
    load_z.wait()

    def gate(chunk, carry):
        lanes = lanes_of(chunk, 256)
        zs = jnp.dot(rearranged, zv[:, lanes], preferred_element_type=F32)
        gz[:, lanes] = silu(zs)
        return carry

    lax.fori_loop(0, DI // 256, gate, 0)
    from_sibling(2)
    for i in range(DI // CH):
        wba[:, CH * i : CH * (i + 1)] = gwb[i].astype(F32)
    sent_tail.wait_recv()
    came = trecv[...].astype(F32)
    opening = jnp.full(came.shape, f, jnp.int32) == 0
    gt[NBF] = jnp.where(opening, 0.0, came).astype(BF16)
    for b in range(2):
        at = where_to[2 * s + b]
        before = jnp.where(at == 0, NBF, order[jnp.maximum(at - 1, 0)])
        halo = gt[before].astype(F32)
        for t in range(KC - 1):
            for j in range(TILES):
                line = halo[t * TILES + j : t * TILES + j + 1]
                xf[b, 5 + t : 6 + t, LANES * j : LANES * (j + 1)] = line

    def heads(tile, carry):
        lanes = lanes_of(tile)
        for b in range(2):
            sigt[BLK * b : BLK * b + 16, lanes] = filtered(b, 16, lanes)
        return carry

    lax.fori_loop(0, TILES, heads, 0)

    def rearrange(chunk, carry):
        lanes = lanes_of(chunk, 256)
        signal[:, lanes] = jnp.dot(rearranged, sigt[:, lanes], preferred_element_type=F32)
        return carry

    lax.fori_loop(0, DI // 256, rearrange, 0)
    proj = lax.dot_general(
        signal[...].astype(BF16),
        wba[DTR:WB].astype(BF16),
        (((1,), (1,)), ((), ())),
        preferred_element_type=F32,
    )
    spread_columns(proj, DTR, in_b)
    rank = proj[:, :DTR]
    high = rank.astype(BF16)
    rest = rank - high.astype(F32)
    mid = rest.astype(BF16)
    low = (rest - mid.astype(F32)).astype(BF16)

    def steps(chunk, carry):
        lanes = lanes_of(chunk, 256)
        weight = wba[0:DTR, lanes].astype(BF16)
        total = wfa[5:6, lanes] + jnp.dot(low, weight, preferred_element_type=F32)
        total = total + jnp.dot(mid, weight, preferred_element_type=F32)
        total = total + jnp.dot(high, weight, preferred_element_type=F32)
        step[:, lanes] = jnp.maximum(total, 0.0) + jnp.log1p(jnp.exp(-jnp.abs(total)))
        return carry

    lax.fori_loop(0, DI // 256, steps, 0)
    m1 = sub % 4 >= 1
    m2 = sub % 4 >= 2

    def rows_of(t):
        return pl.ds(pl.multiple_of(t * CHUNKS, CHUNKS), CHUNKS)

    def rates_of(lanes):
        return [jnp.broadcast_to(rate2[n : n + 1, lanes], full) for n in range(NS)]

    def block_states(tile, carry):
        lanes = lanes_of(tile)
        rates = rates_of(lanes)

        def one(t, held):
            states, total = held
            rows = rows_of(t)
            now = step[rows, lanes]
            drive = now * signal[rows, lanes]
            states = tuple(
                jnp.exp2(now * rates[n]) * states[n] + in_b[n, rows, :] * drive for n in range(NS)
            )
            return states, total + now

        states, total = lax.fori_loop(0, STEPS, one, ((zero,) * NS, zero), unroll=4)
        sum1 = total + jnp.where(m1, pltpu.roll(total, 1, 0), 0.0)
        sum2 = sum1 + jnp.where(m2, pltpu.roll(sum1, 2, 0), 0.0)
        reach[:, lanes] = jnp.where(m1, pltpu.roll(sum2, 1, 0), 0.0)
        ends = jnp.where(
            sub < 4, jnp.broadcast_to(sum2[3:4], full), jnp.broadcast_to(sum2[7:8], full)
        )
        group = tile // 3
        place = tile % 3
        for h in range(4):
            state_out = zero
            rate_out = zero
            for q in range(4):
                n = 4 * h + q
                decay = jnp.exp2(rates[n] * total)
                one_s = states[n] + jnp.where(m1, decay * pltpu.roll(states[n], 1, 0), 0.0)
                decay2 = jnp.exp2(rates[n] * sum1)
                two_s = one_s + jnp.where(m2, decay2 * pltpu.roll(one_s, 2, 0), 0.0)
                inner[n, :, lanes] = jnp.where(m1, pltpu.roll(two_s, 1, 0), 0.0)
                turn = (q + 5) % 8
                moved = pltpu.roll(two_s, turn, 0) if turn else two_s
                state_out = jnp.where(sub % 4 == q, moved, state_out)
                rate_out = jnp.where(sub % 4 == q, rates[n], rate_out)
            sends[group * 4 + h, place] = state_out
            sends[group * 4 + h, 3] = jnp.where(sub % 4 == place, ends, sends[group * 4 + h, 3])
            rate_own[h, tile] = rate_out
        return carry

    def to_owner(peer):
        return remote(sends.at[peer], recv.at[s], sa.at[peer], ra.at[s], (f, peer))

    def one_group(g, carry):
        lax.fori_loop(g * 3, g * 3 + 3, block_states, 0)
        for h in range(4):
            peer = g * 4 + h

            @pl.when(peer != s)
            def _():
                to_owner(peer).start()

        return carry

    lax.fori_loop(0, 4, one_group, 0)
    recv[s] = sends[s]
    spread_columns(proj, DTR + NS, out_b)

    def own_outputs(tile, carry):
        lanes = lanes_of(tile)
        rates = rates_of(lanes)
        skip = jnp.broadcast_to(wfa[6:7, lanes], full)

        def one(t, held):
            states, total = held
            rows = rows_of(t)
            now = step[rows, lanes]
            sig = signal[rows, lanes]
            drive = now * sig
            total = total + now
            states = tuple(
                jnp.exp2(now * rates[n]) * states[n] + in_b[n, rows, :] * drive for n in range(NS)
            )
            coeffs = [out_b[n, rows, :] for n in range(NS)]
            terms = [coeffs[n] * states[n] for n in range(NS)]
            for n in range(NS):
                grown[n, rows, lanes] = coeffs[n] * jnp.exp2(total * rates[n])
            while len(terms) > 1:
                terms = [a + b for a, b in zip(terms[::2], terms[1::2])]
            y[rows, lanes] = terms[0] + skip * sig
            return states, total

        states = tuple(inner[n, :, lanes] for n in range(NS))
        lax.fori_loop(0, STEPS, one, (states, reach[:, lanes]), unroll=2)
        return carry

    lax.fori_loop(0, 3, own_outputs, 0)
    for d in range(1, width):
        peer = (s + d) % width
        remote(sends.at[peer], recv.at[peer], sa.at[peer], ra.at[peer], (f, peer)).wait_recv()

    def turned(v):
        return pltpu.roll(v, 4, len(v.shape) - 2)

    my_group = s // 4
    my_rates = rate_own[s % 4, pl.ds(my_group * 3, 3)]

    def through(j, carry):
        e, p = carry
        scan_e[j] = e
        scan_p[j] = p
        block = order[j]
        got = recv[lax.shift_right_logical(block, 1)]
        odd = jnp.full((4, CHUNKS, LANES), block & 1, jnp.int32) == 1
        got = jnp.where(odd, turned(got), got)
        sums = jnp.stack([jnp.broadcast_to(got[3, i : i + 1], full) for i in range(3)])
        a = jnp.exp2(my_rates * sums)
        return a * e + got[0:3], a * p

    zero3 = jnp.zeros(slot, F32)
    unit3 = jnp.ones(slot, F32)
    e, p = lax.fori_loop(0, NBF, through, (zero3, unit3), unroll=8)
    pk1[...] = jnp.where(sub3 < 4, p, turned(e))
    got1[seat] = pk1[...]
    level1 = []
    for d in range(1, SEATS):
        level1.append(push(pk1, got1.at[seat], sb1.at[d], rb1.at[d], (near(d), s)))
    lax.fori_loop(3, 6, own_outputs, 0)
    for copy in level1:
        copy.wait_recv()

    def gather_near(m, carry):
        e_in, p_in, e_all, p_all = carry
        got = got1[m]
        moved = turned(got)
        early = jnp.full(slot, m, jnp.int32) < jnp.full(slot, seat, jnp.int32)
        e_in = jnp.where(early, got * e_in + moved, e_in)
        p_in = jnp.where(early, got * p_in, p_in)
        return e_in, p_in, got * e_all + moved, got * p_all

    begin = (zero3, unit3, zero3, unit3)
    e_in, p_in, e_all, p_all = lax.fori_loop(0, SEATS, gather_near, begin, unroll=SEATS)
    pk2[...] = jnp.where(sub3 < 4, p_all, turned(e_all))
    got2[part] = pk2[...]
    level2 = []
    for d in range(1, outer):
        level2.append(push(pk2, got2.at[part], sc.at[d], rc.at[d], (far(d), s)))
    lax.fori_loop(6, 9, own_outputs, 0)
    for copy in level2:
        copy.wait_recv()

    def gather_far(m, start):
        got = got2[m]
        early = jnp.full(slot, m, jnp.int32) < jnp.full(slot, part, jnp.int32)
        return jnp.where(early, got * start + turned(got), start)

    start = lax.fori_loop(0, outer, gather_far, zero3, unroll=4)
    start = p_in * start + e_in

    def pack(d, carry):
        i0 = where_to[2 * d]
        i1 = where_to[2 * d + 1]
        even = scan_e[i0] + scan_p[i0] * start
        odd = scan_e[i1] + scan_p[i1] * start
        bsend[d] = jnp.where(sub3 < 4, even, turned(odd))
        return carry

    lax.fori_loop(0, width, pack, 0, unroll=4)
    back[s] = bsend[s]
    returns = []
    for d in range(1, width):
        peer = (s + d) % width
        returns.append(push(bsend.at[peer], back.at[s], sd.at[peer], rd.at[s], (f, peer)))
    lax.fori_loop(9, 12, own_outputs, 0)
    load_ow.wait()
    def complete(tile, carry):
        lanes = lanes_of(tile)
        group = tile // 3
        place = tile % 3
        entering = []
        for n in range(NS):
            came = back[group * 4 + n // 4, place]
            q = n % 4
            entering.append(
                jnp.where(
                    sub < 4,
                    jnp.broadcast_to(came[q : q + 1], full),
                    jnp.broadcast_to(came[4 + q : 5 + q], full),
                )
            )

        def one(t, carry):
            rows = rows_of(t)
            terms = [grown[n, rows, lanes] * entering[n] for n in range(NS)]
            while len(terms) > 1:
                terms = [a + b for a, b in zip(terms[::2], terms[1::2])]
            scanned = (y[rows, lanes] + terms[0]).astype(BF16).astype(F32)
            y[rows, lanes] = scanned * gz[rows, lanes]
            return carry

        lax.fori_loop(0, STEPS, one, 0, unroll=4)
        gated[:, lanes] = y[:, lanes].astype(BF16)
        return carry

    def one_return(g, carry):
        for h in range(4):
            peer = g * 4 + h

            @pl.when(peer != s)
            def _():
                remote(
                    bsend.at[peer], back.at[peer], sd.at[peer], rd.at[peer], (f, peer)
                ).wait_recv()

        lax.fori_loop(g * 3, g * 3 + 3, complete, 0)
        return carry

    lax.fori_loop(0, 4, one_return, 0)
    undo = token_rows()

    def mix(chunk, carry):
        lanes = lanes_of(chunk, 256)
        mixed = jnp.dot(gated[...], owv[:, lanes], preferred_element_type=F32).astype(BF16)
        out[:, lanes] = jnp.dot(undo, mixed, preferred_element_type=F32).astype(BF16)
        return carry

    lax.fori_loop(0, D // 256, mix, 0)
    for copy in sent + level1 + level2 + returns:
        copy.wait_send()
    for d in range(1, width):
        to_owner((s + d) % width).wait_send()


def shards(
    inner_x,
    inner_z,
    conv_weight,
    conv_bias,
    proj_weight,
    step_weight,
    step_bias,
    decay_log,
    skip_gain,
    out_weight,
    order_table,
):
    frames, rows, columns, channels = inner_x.shape
    space = lax.axis_size("space")
    outer = lax.axis_size("tm") // SEATS
    dma = pltpu.SemaphoreType.DMA
    slot = (3, CHUNKS, LANES)
    anyw = pl.BlockSpec(memory_space=pl.ANY)
    vm = pl.BlockSpec(memory_space=pltpu.VMEM)
    held = [
        ((TOK, DI), BF16),
        ((TOK, DI), BF16),
        ((DI, D), BF16),
        ((space, WROWS, CH), F32),
        ((space, WB, CH), BF16),
        ((NBF + 1, TROWS, LANES), BF16),
        ((2, TROWS, LANES), F32),
        ((TROWS, LANES), BF16),
        ((TROWS, LANES), BF16),
        None,
        ((WROWS, DI), F32),
        ((WB, DI), F32),
        ((2, BLK + 8, DI), F32),
        ((TOK, DI), BF16),
        ((TOK, DI), F32),
        ((TOK, DI), F32),
        ((TOK, DI), F32),
        ((NS, DI), F32),
        ((4, TILES, CHUNKS, LANES), F32),
        ((NS, TOK, LANES), F32),
        ((NS, TOK, LANES), F32),
        ((NS, CHUNKS, DI), F32),
        ((CHUNKS, DI), F32),
        ((TOK, DI), F32),
        ((TOK, DI), BF16),
        ((NS, TOK, DI), F32),
        ((space, 4, CHUNKS, LANES), F32),
        ((space, 4, CHUNKS, LANES), F32),
        ((NBF,) + slot, F32),
        ((NBF,) + slot, F32),
        (slot, F32),
        ((SEATS,) + slot, F32),
        (slot, F32),
        ((outer,) + slot, F32),
        ((space,) + slot, F32),
        ((space,) + slot, F32),
    ]
    scratch = [pltpu.SMEM((NBF,), jnp.int32) if h is None else pltpu.VMEM(*h) for h in held]
    scratch += [dma((3,))] + [dma((3, 8))] * 4 + [dma] * 2
    scratch += [dma((16,))] * 2 + [dma((8,))] * 4 + [dma((16,))] * 2
    out = pl.pallas_call(
        layer,
        out_shape=jax.ShapeDtypeStruct((TOK, D), BF16),
        in_specs=[anyw, anyw] + [vm] * 7 + [anyw, pl.BlockSpec(memory_space=pltpu.SMEM)],
        out_specs=vm,
        scratch_shapes=scratch,
        compiler_params=pltpu.CompilerParams(
            collective_id=0, has_side_effects=True, vmem_limit_bytes=VMEM_LIMIT
        ),
        name="layer",
    )(
        inner_x.reshape(TOK, DI),
        inner_z.reshape(TOK, DI),
        conv_weight,
        conv_bias.reshape(1, CH),
        proj_weight.T,
        step_weight,
        step_bias.reshape(1, CH),
        decay_log,
        skip_gain.reshape(1, CH),
        out_weight,
        order_table,
    )
    return out.reshape(frames, rows, columns, D)


def solution(mesh):
    in_specs = (
        P("tm", "space", None, None),
        P("tm", "space", None, None),
        P(None, "space"),
        P("space"),
        P("space", None),
        P(None, "space"),
        P("space"),
        P(None, "space"),
        P("space"),
        P(),
        P(),
    )
    out_specs = P("tm", "space", None, None)
    return jax.shard_map(shards, mesh=mesh, in_specs=in_specs, out_specs=out_specs, check_vma=False)
```

```python
import jax
import jax.numpy as jnp
from jax import lax
from jax.experimental import pallas as pl
from jax.experimental.pallas import tpu as pltpu
from jax.sharding import PartitionSpec as P

MESH = pl.DeviceIdType.MESH
NS = 16
DTR = 48
KC = 4
BLK = 128
NBF = 32
DI = 1536
D = 768
TOK = 256
CH = 96
LANES = 128
TILES = DI // LANES
CHUNKS = 8
STEPS = TOK // CHUNKS
WROWS = 24
TROWS = 48
WB = DTR + DTR + 2 * NS
SEATS = 8
VMEM_LIMIT = 56 * 1024 * 1024
LOG2E = 1.4426950408889634
F32 = jnp.float32
BF16 = jnp.bfloat16


def scan_rows():
    r = lax.broadcasted_iota(jnp.int32, (TOK, TOK), 0)
    i = lax.broadcasted_iota(jnp.int32, (TOK, TOK), 1)
    return ((r & (CHUNKS - 1)) * STEPS + (r >> 3) == i).astype(F32).astype(BF16)


def token_rows():
    i = lax.broadcasted_iota(jnp.int32, (TOK, TOK), 0)
    r = lax.broadcasted_iota(jnp.int32, (TOK, TOK), 1)
    return ((r & (CHUNKS - 1)) * STEPS + (r >> 3) == i).astype(F32).astype(BF16)


def silu(v):
    half = 0.5 * v
    return half + half * jnp.tanh(half)


def lanes_of(tile, width=LANES):
    return pl.ds(pl.multiple_of(tile * width, width), width)


def spread_columns(projected, first, out):
    for n in range(NS):
        out[n] = jnp.broadcast_to(projected[:, first + n : first + n + 1], (TOK, LANES))


def layer(
    x, z, cw, cb, pwt, sw, sb, dl, sg, order, out,
    xv, zv, gwf, gwb, gt, tstage, tsend, trecv, where_to,
    wfa, wba, xf, sigt, gz, signal, step, rate2, rate_own, in_b, out_b, inner, reach, y, gated, grown,
    sends, recv, scan_e, scan_t, pk1, got1, pk2, got2, bsend, back, fsend, fback,
    local, s1, r1, s2, r2, st, rt, sa, ra, sb1, rb1, sc, rc, sd, rd, sf, rf,
):
    f = lax.axis_index("tm")
    s = lax.axis_index("space")
    frames = lax.axis_size("tm")
    width = lax.axis_size("space")
    outer = frames // SEATS
    row = s // 4
    side = s // 2 % 2
    core = s % 2
    part = f // SEATS
    seat = f % SEATS
    sibling = (f, s - core + 1 - core)
    twin = f + 1 - f % 2 * 2
    ahead = ((f + 1) % frames, s)
    behind = ((f + frames - 1) % frames, s)
    full = (CHUNKS, LANES)
    slot = (3, CHUNKS, LANES)
    sub = lax.broadcasted_iota(jnp.int32, full, 0)
    sub3 = lax.broadcasted_iota(jnp.int32, slot, 1)
    zero = jnp.zeros(full, F32)

    def chip(dx, dy):
        return (row + dx) % 4 * 4 + (side + dy) % 2 * 2 + core

    def near(d):
        return part * SEATS + (seat + d) % SEATS

    def far(d):
        return ((part + d) % outer) * SEATS + seat

    def remote(src, dst, ssem, rsem, target):
        return pltpu.make_async_remote_copy(
            src_ref=src,
            dst_ref=dst,
            send_sem=ssem,
            recv_sem=rsem,
            device_id=target,
            device_id_type=MESH,
        )

    def push(src, dst, ssem, rsem, target):
        copy = remote(src, dst, ssem, rsem, target)
        copy.start()
        return copy

    load_x = pltpu.make_async_copy(x, xv, local.at[0])
    load_z = pltpu.make_async_copy(z, zv, local.at[1])
    load_x.start()

    barrier = pltpu.get_barrier_semaphore()
    for d in range(1, width):
        pl.semaphore_signal(barrier, inc=1, device_id=(f, (s + d) % width), device_id_type=MESH)
    for d in range(1, SEATS):
        pl.semaphore_signal(barrier, inc=1, device_id=(near(d), s), device_id_type=MESH)
    for d in range(1, outer):
        pl.semaphore_signal(barrier, inc=1, device_id=(far(d), s), device_id_type=MESH)
    pl.semaphore_signal(barrier, inc=1, device_id=behind, device_id_type=MESH)
    for dx in range(4):
        pl.semaphore_signal(barrier, inc=1, device_id=(twin, chip(dx, 1)), device_id_type=MESH)

    load_z.start()
    gwf[s, 0:KC] = cw[...]
    gwf[s, KC : KC + 1] = cb[...]
    gwf[s, 5:6] = sb[...]
    gwf[s, 6:7] = sg[...]
    gwf[s, 7:8] = jnp.zeros((1, CH), F32)
    gwf[s, 8:WROWS] = dl[...]
    gwb[s, 0:DTR] = sw[...]
    gwb[s, DTR:WB] = pwt[...]
    tstage[...] = jnp.zeros_like(tstage)
    load_x.wait()
    for b in range(2):
        ends = xv[BLK * (b + 1) - 16 : BLK * (b + 1)].astype(F32)
        for t in range(KC - 1):
            for j in range(TILES):
                line = ends[13 + t : 14 + t, LANES * j : LANES * (j + 1)]
                tstage[b, t * TILES + j : t * TILES + j + 1] = line
    gt[pl.ds(2 * s, 2)] = tstage[...].astype(BF16)
    pl.semaphore_wait(barrier, width + SEATS + outer + 2)

    def place(a, i):
        return (gwf.at[i], gt.at[pl.ds(2 * i, 2)], gwb.at[i])[a]

    sent = []
    relayed = [0, 0, 0]

    def relay(a, dx, dy, tx, ty):
        ref = place(a, chip(dx, dy))
        landing = (dx - tx) % 4 * 2 + (dy - ty) % 2
        ssem = s1.at[a, relayed[a]]
        relayed[a] += 1
        frame = twin if ty and a != 1 else f
        sent.append(push(ref, ref, ssem, r1.at[a, landing], (frame, chip(tx, ty))))

    def share(a, dx, dy):
        ref = place(a, chip(dx, dy))
        k = dx * 2 + dy
        sent.append(push(ref, ref, s2.at[a, k], r2.at[a, k], sibling))

    def take(a, dx, dy):
        ref = place(a, chip(dx, dy))
        remote(ref, ref, s1.at[a, 0], r1.at[a, dx * 2 + dy], sibling).wait_recv()

    def offer(a):
        for tx, ty in ((1, 0), (3, 0), (0, 1), (1, 1), (3, 1), (2, 0), (2, 1)):
            relay(a, 0, 0, tx, ty)
        share(a, 0, 0)

    def collect(a):
        for dx, dy in ((3, 0), (1, 0), (0, 1), (3, 1), (1, 1), (2, 0), (2, 1)):
            take(a, dx, dy)
            share(a, dx, dy)

    def own_item(a):
        relay(a, 0, 0, 1, 0)
        relay(a, 0, 0, 3, 0)
        relay(a, 0, 0, 0, 1)
        share(a, 0, 0)

    def other_side(a):
        take(a, 0, 1)
        relay(a, 0, 1, 1, 0)
        relay(a, 0, 1, 3, 0)
        share(a, 0, 1)

    def neighbours(a):
        for dy in range(2):
            take(a, 1, dy)
            relay(a, 1, dy, 3, 0)
            share(a, 1, dy)
        for dy in range(2):
            take(a, 3, dy)
            share(a, 3, dy)

    def opposite(a):
        for dy in range(2):
            take(a, 2, dy)
            share(a, 2, dy)

    def from_sibling(a):
        for dx in range(4):
            for dy in range(2):
                ref = place(a, chip(dx, dy) - core + 1 - core)
                k = dx * 2 + dy
                remote(ref, ref, s2.at[a, k], r2.at[a, k], sibling).wait_recv()

    offer(0)
    offer(1)
    own_item(2)
    listed = [order[j] for j in range(NBF)]

    def inverse(r, carry):
        found = 0
        for j in range(NBF):
            found = jnp.where(listed[j] == r, j, found)
        where_to[r] = found
        return carry

    lax.fori_loop(0, NBF, inverse, 0)
    for b in range(2):
        xf[b, 0:8] = jnp.zeros((8, DI), F32)

    def widen(tile, carry):
        lanes = lanes_of(tile)
        for b in range(2):
            xf[b, 8 : 8 + BLK, lanes] = xv[BLK * b : BLK * (b + 1), lanes].astype(F32)
        return carry

    lax.fori_loop(0, TILES, widen, 0)
    sends[...] = jnp.zeros_like(sends)
    collect(0)
    other_side(2)
    collect(1)
    from_sibling(0)
    for i in range(DI // CH):
        wfa[:, CH * i : CH * (i + 1)] = gwf[i]

    def filtered(b, count, lanes):
        total = wfa[4:5, lanes]
        for k in range(KC):
            total = total + wfa[k : k + 1, lanes] * xf[b, 5 + k : 5 + k + count, lanes]
        return silu(total).astype(BF16)

    def convolve(tile, carry):
        lanes = lanes_of(tile)
        for b in range(2):
            sigt[BLK * b : BLK * (b + 1), lanes] = filtered(b, BLK, lanes)
        return carry

    lax.fori_loop(0, 3, convolve, 0)
    neighbours(2)
    lax.fori_loop(3, 6, convolve, 0)
    from_sibling(1)
    tsend[...] = gt[order[NBF - 1]]
    sent_tail = push(tsend, trecv, st, rt, ahead)
    sent.append(sent_tail)
    opposite(2)
    lax.fori_loop(6, TILES, convolve, 0)
    rate2[...] = -jnp.exp(wfa[8:WROWS]) * LOG2E
    rearranged = scan_rows()
    load_z.wait()

    def gate(chunk, carry):
        lanes = lanes_of(chunk, 256)
        zs = jnp.dot(rearranged, zv[:, lanes], preferred_element_type=F32)
        gz[:, lanes] = silu(zs)
        return carry

    lax.fori_loop(0, DI // 256, gate, 0)
    from_sibling(2)
    for i in range(DI // CH):
        wba[:, CH * i : CH * (i + 1)] = gwb[i].astype(F32)
    sent_tail.wait_recv()
    came = trecv[...].astype(F32)
    opening = jnp.full(came.shape, f, jnp.int32) == 0
    gt[NBF] = jnp.where(opening, 0.0, came).astype(BF16)
    for b in range(2):
        at = where_to[2 * s + b]
        before = jnp.where(at == 0, NBF, order[jnp.maximum(at - 1, 0)])
        halo = gt[before].astype(F32)
        for t in range(KC - 1):
            for j in range(TILES):
                line = halo[t * TILES + j : t * TILES + j + 1]
                xf[b, 5 + t : 6 + t, LANES * j : LANES * (j + 1)] = line

    def heads(tile, carry):
        lanes = lanes_of(tile)
        for b in range(2):
            sigt[BLK * b : BLK * b + 16, lanes] = filtered(b, 16, lanes)
        return carry

    lax.fori_loop(0, TILES, heads, 0)

    def rearrange(chunk, carry):
        lanes = lanes_of(chunk, 256)
        signal[:, lanes] = jnp.dot(rearranged, sigt[:, lanes], preferred_element_type=F32)
        return carry

    lax.fori_loop(0, DI // 256, rearrange, 0)
    proj = lax.dot_general(
        signal[...].astype(BF16),
        wba[DTR:WB].astype(BF16),
        (((1,), (1,)), ((), ())),
        preferred_element_type=F32,
    )
    spread_columns(proj, DTR, in_b)
    rank = proj[:, :DTR]
    high = rank.astype(BF16)
    rest = rank - high.astype(F32)
    mid = rest.astype(BF16)
    low = (rest - mid.astype(F32)).astype(BF16)

    def steps(chunk, carry):
        lanes = lanes_of(chunk, 256)
        weight = wba[0:DTR, lanes].astype(BF16)
        total = wfa[5:6, lanes] + jnp.dot(low, weight, preferred_element_type=F32)
        total = total + jnp.dot(mid, weight, preferred_element_type=F32)
        total = total + jnp.dot(high, weight, preferred_element_type=F32)
        step[:, lanes] = jnp.maximum(total, 0.0) + jnp.log1p(jnp.exp(-jnp.abs(total)))
        return carry

    lax.fori_loop(0, DI // 256, steps, 0)
    m1 = sub % 4 >= 1
    m2 = sub % 4 >= 2

    def rows_of(t):
        return pl.ds(pl.multiple_of(t * CHUNKS, CHUNKS), CHUNKS)

    def rates_of(lanes):
        return [jnp.broadcast_to(rate2[n : n + 1, lanes], full) for n in range(NS)]

    def block_states(tile, carry):
        lanes = lanes_of(tile)
        rates = rates_of(lanes)

        def one(t, held):
            states, total = held
            rows = rows_of(t)
            now = step[rows, lanes]
            drive = now * signal[rows, lanes]
            states = tuple(
                jnp.exp2(now * rates[n]) * states[n] + in_b[n, rows, :] * drive for n in range(NS)
            )
            return states, total + now

        states, total = lax.fori_loop(0, STEPS, one, ((zero,) * NS, zero), unroll=4)
        sum1 = total + jnp.where(m1, pltpu.roll(total, 1, 0), 0.0)
        sum2 = sum1 + jnp.where(m2, pltpu.roll(sum1, 2, 0), 0.0)
        reach[:, lanes] = jnp.where(m1, pltpu.roll(sum2, 1, 0), 0.0)
        ends = jnp.where(
            sub < 4, jnp.broadcast_to(sum2[3:4], full), jnp.broadcast_to(sum2[7:8], full)
        )
        group = tile // 3
        place = tile % 3
        for h in range(4):
            state_out = zero
            rate_out = zero
            for q in range(4):
                n = 4 * h + q
                decay = jnp.exp2(rates[n] * total)
                one_s = states[n] + jnp.where(m1, decay * pltpu.roll(states[n], 1, 0), 0.0)
                decay2 = jnp.exp2(rates[n] * sum1)
                two_s = one_s + jnp.where(m2, decay2 * pltpu.roll(one_s, 2, 0), 0.0)
                inner[n, :, lanes] = jnp.where(m1, pltpu.roll(two_s, 1, 0), 0.0)
                turn = (q + 5) % 8
                moved = pltpu.roll(two_s, turn, 0) if turn else two_s
                state_out = jnp.where(sub % 4 == q, moved, state_out)
                rate_out = jnp.where(sub % 4 == q, rates[n], rate_out)
            sends[group * 4 + h, place] = state_out
            sends[group * 4 + h, 3] = jnp.where(sub % 4 == place, ends, sends[group * 4 + h, 3])
            rate_own[h, tile] = rate_out
        return carry

    def to_owner(peer):
        return remote(sends.at[peer], recv.at[s], sa.at[peer], ra.at[s], (f, peer))

    def one_group(g, carry):
        lax.fori_loop(g * 3, g * 3 + 3, block_states, 0)
        for h in range(4):
            peer = g * 4 + h

            @pl.when(peer != s)
            def _():
                to_owner(peer).start()

        return carry

    lax.fori_loop(0, 4, one_group, 0)
    recv[s] = sends[s]
    spread_columns(proj, DTR + NS, out_b)

    def own_outputs(tile, carry):
        lanes = lanes_of(tile)
        rates = rates_of(lanes)
        skip = jnp.broadcast_to(wfa[6:7, lanes], full)

        def one(t, held):
            states, total = held
            rows = rows_of(t)
            now = step[rows, lanes]
            sig = signal[rows, lanes]
            drive = now * sig
            total = total + now
            states = tuple(
                jnp.exp2(now * rates[n]) * states[n] + in_b[n, rows, :] * drive for n in range(NS)
            )
            coeffs = [out_b[n, rows, :] for n in range(NS)]
            terms = [coeffs[n] * states[n] for n in range(NS)]
            for n in range(NS):
                grown[n, rows, lanes] = coeffs[n] * jnp.exp2(total * rates[n])
            while len(terms) > 1:
                terms = [a + b for a, b in zip(terms[::2], terms[1::2])]
            y[rows, lanes] = terms[0] + skip * sig
            return states, total

        states = tuple(inner[n, :, lanes] for n in range(NS))
        lax.fori_loop(0, STEPS, one, (states, reach[:, lanes]), unroll=2)
        return carry

    lax.fori_loop(0, 3, own_outputs, 0)
    for d in range(1, width):
        peer = (s + d) % width
        remote(sends.at[peer], recv.at[peer], sa.at[peer], ra.at[peer], (f, peer)).wait_recv()

    def turned(v):
        return pltpu.roll(v, 4, len(v.shape) - 2)

    my_group = s // 4
    my_rates = rate_own[s % 4, pl.ds(my_group * 3, 3)]

    def decays(sums):
        spread = [jnp.broadcast_to(sums[i : i + 1], full) for i in range(3)]
        return jnp.exp2(my_rates * jnp.stack(spread))

    def through(j, carry):
        e, passed = carry
        scan_e[j] = e
        scan_t[j] = passed
        block = order[j]
        got = recv[lax.shift_right_logical(block, 1)]
        odd = jnp.full((4, CHUNKS, LANES), block & 1, jnp.int32) == 1
        got = jnp.where(odd, turned(got), got)
        return decays(got[3]) * e + got[0:3], passed + got[3]

    zero3 = jnp.zeros(slot, F32)
    unit3 = jnp.ones(slot, F32)
    e, passed = lax.fori_loop(0, NBF, through, (zero3, zero), unroll=8)
    p = decays(passed)
    pk1[...] = jnp.where(sub3 < 4, p, turned(e))
    got1[seat] = pk1[...]
    level1 = []
    for d in range(1, SEATS):
        level1.append(push(pk1, got1.at[seat], sb1.at[d], rb1.at[d], (near(d), s)))

    def pack(d, carry):
        i0 = where_to[2 * d]
        i1 = where_to[2 * d + 1]
        bsend[d, 0:3] = jnp.where(sub3 < 4, scan_e[i0], turned(scan_e[i1]))
        bsend[d, 3] = jnp.where(sub < 4, scan_t[i0], turned(scan_t[i1]))
        return carry

    lax.fori_loop(0, width, pack, 0, unroll=4)
    back[s] = bsend[s]
    returns = []
    for d in range(1, width):
        peer = (s + d) % width
        returns.append(push(bsend.at[peer], back.at[s], sd.at[peer], rd.at[s], (f, peer)))
    lax.fori_loop(3, 6, own_outputs, 0)
    for copy in level1:
        copy.wait_recv()

    def gather_near(m, carry):
        e_in, p_in, e_all, p_all = carry
        got = got1[m]
        moved = turned(got)
        early = jnp.full(slot, m, jnp.int32) < jnp.full(slot, seat, jnp.int32)
        e_in = jnp.where(early, got * e_in + moved, e_in)
        p_in = jnp.where(early, got * p_in, p_in)
        return e_in, p_in, got * e_all + moved, got * p_all

    begin = (zero3, unit3, zero3, unit3)
    e_in, p_in, e_all, p_all = lax.fori_loop(0, SEATS, gather_near, begin, unroll=SEATS)
    pk2[...] = jnp.where(sub3 < 4, p_all, turned(e_all))
    got2[part] = pk2[...]
    level2 = []
    for d in range(1, outer):
        level2.append(push(pk2, got2.at[part], sc.at[d], rc.at[d], (far(d), s)))
    lax.fori_loop(6, 9, own_outputs, 0)
    for copy in level2:
        copy.wait_recv()

    def gather_far(m, start):
        got = got2[m]
        early = jnp.full(slot, m, jnp.int32) < jnp.full(slot, part, jnp.int32)
        return jnp.where(early, got * start + turned(got), start)

    start = lax.fori_loop(0, outer, gather_far, zero3, unroll=4)
    start = p_in * start + e_in

    first = jnp.where(sub < 4, start[0], turned(start[1]))
    fsend[...] = jnp.concatenate([first, start[2]], axis=0).astype(BF16)
    fback[s] = fsend[...]
    starts = []
    for d in range(1, width):
        peer = (s + d) % width
        starts.append(push(fsend, fback.at[s], sf.at[peer], rf.at[s], (f, peer)))
    lax.fori_loop(9, 12, own_outputs, 0)
    for d in range(1, width):
        peer = (s + d) % width
        remote(bsend.at[peer], back.at[peer], sd.at[peer], rd.at[peer], (f, peer)).wait_recv()

    def both(tile8, r):
        return jnp.where(
            sub < 4,
            jnp.broadcast_to(tile8[r : r + 1], full),
            jnp.broadcast_to(tile8[4 + r : 5 + r], full),
        )

    def complete(g, place):
        lanes = lanes_of(g * 3 + place)
        rates = rates_of(lanes)
        passed = both(back[g * 4, 3], place)
        entering = []
        for h in range(4):
            came = back[g * 4 + h, place]
            begun = fback[g * 4 + h].astype(F32)
            for q in range(4):
                r = place * 4 + q
                line = jnp.broadcast_to(begun[r : r + 1], full)
                entering.append(both(came, q) + jnp.exp2(rates[4 * h + q] * passed) * line)

        def one(t, carry):
            rows = rows_of(t)
            terms = [grown[n, rows, lanes] * entering[n] for n in range(NS)]
            while len(terms) > 1:
                terms = [a + b for a, b in zip(terms[::2], terms[1::2])]
            scanned = (y[rows, lanes] + terms[0]).astype(BF16).astype(F32)
            y[rows, lanes] = scanned * gz[rows, lanes]
            return carry

        lax.fori_loop(0, STEPS, one, 0, unroll=4)
        gated[:, lanes] = y[:, lanes].astype(BF16)

    undo = token_rows()

    def one_group_back(g, carry):
        for h in range(4):
            peer = g * 4 + h

            @pl.when(peer != s)
            def _():
                remote(fsend, fback.at[peer], sf.at[peer], rf.at[peer], (f, peer)).wait_recv()

        for place in range(3):
            complete(g, place)
        lanes = lanes_of(g, 3 * LANES)
        out[:, lanes] = jnp.dot(undo, gated[:, lanes], preferred_element_type=F32).astype(BF16)
        return carry

    lax.fori_loop(0, 4, one_group_back, 0)
    for copy in sent + level1 + level2 + returns + starts:
        copy.wait_send()
    for d in range(1, width):
        to_owner((s + d) % width).wait_send()


def shards(
    inner_x,
    inner_z,
    conv_weight,
    conv_bias,
    proj_weight,
    step_weight,
    step_bias,
    decay_log,
    skip_gain,
    out_weight,
    order_table,
):
    frames, rows, columns, channels = inner_x.shape
    space = lax.axis_size("space")
    outer = lax.axis_size("tm") // SEATS
    dma = pltpu.SemaphoreType.DMA
    slot = (3, CHUNKS, LANES)
    anyw = pl.BlockSpec(memory_space=pl.ANY)
    vm = pl.BlockSpec(memory_space=pltpu.VMEM)
    held = [
        ((TOK, DI), BF16),
        ((TOK, DI), BF16),
        ((space, WROWS, CH), F32),
        ((space, WB, CH), BF16),
        ((NBF + 1, TROWS, LANES), BF16),
        ((2, TROWS, LANES), F32),
        ((TROWS, LANES), BF16),
        ((TROWS, LANES), BF16),
        None,
        ((WROWS, DI), F32),
        ((WB, DI), F32),
        ((2, BLK + 8, DI), F32),
        ((TOK, DI), BF16),
        ((TOK, DI), F32),
        ((TOK, DI), F32),
        ((TOK, DI), F32),
        ((NS, DI), F32),
        ((4, TILES, CHUNKS, LANES), F32),
        ((NS, TOK, LANES), F32),
        ((NS, TOK, LANES), F32),
        ((NS, CHUNKS, DI), F32),
        ((CHUNKS, DI), F32),
        ((TOK, DI), F32),
        ((TOK, DI), BF16),
        ((NS, TOK, DI), F32),
        ((space, 4, CHUNKS, LANES), F32),
        ((space, 4, CHUNKS, LANES), F32),
        ((NBF,) + slot, F32),
        ((NBF, CHUNKS, LANES), F32),
        (slot, F32),
        ((SEATS,) + slot, F32),
        (slot, F32),
        ((outer,) + slot, F32),
        ((space, 4, CHUNKS, LANES), F32),
        ((space, 4, CHUNKS, LANES), F32),
        ((16, LANES), BF16),
        ((space, 16, LANES), BF16),
    ]
    scratch = [pltpu.SMEM((NBF,), jnp.int32) if h is None else pltpu.VMEM(*h) for h in held]
    scratch += [dma((2,))] + [dma((3, 8))] * 4 + [dma] * 2
    scratch += [dma((16,))] * 2 + [dma((8,))] * 4 + [dma((16,))] * 4
    gated = pl.pallas_call(
        layer,
        out_shape=jax.ShapeDtypeStruct((TOK, DI), BF16),
        in_specs=[anyw, anyw] + [vm] * 7 + [pl.BlockSpec(memory_space=pltpu.SMEM)],
        out_specs=vm,
        scratch_shapes=scratch,
        compiler_params=pltpu.CompilerParams(
            collective_id=0, has_side_effects=True, vmem_limit_bytes=VMEM_LIMIT
        ),
        name="layer",
    )(
        inner_x.reshape(TOK, DI),
        inner_z.reshape(TOK, DI),
        conv_weight,
        conv_bias.reshape(1, CH),
        proj_weight.T,
        step_weight,
        step_bias.reshape(1, CH),
        decay_log,
        skip_gain.reshape(1, CH),
        order_table,
    )
    mixed = jnp.dot(gated, out_weight, preferred_element_type=F32).astype(BF16)
    return mixed.reshape(frames, rows, columns, D)


def solution(mesh):
    in_specs = (
        P("tm", "space", None, None),
        P("tm", "space", None, None),
        P(None, "space"),
        P("space"),
        P("space", None),
        P(None, "space"),
        P("space"),
        P(None, "space"),
        P("space"),
        P(),
        P(),
    )
    out_specs = P("tm", "space", None, None)
    return jax.shard_map(shards, mesh=mesh, in_specs=in_specs, out_specs=out_specs, check_vma=False)
```

```python
import jax
import jax.numpy as jnp
from jax import lax
from jax.experimental import pallas as pl
from jax.experimental.pallas import tpu as pltpu
from jax.sharding import PartitionSpec as P

MESH = pl.DeviceIdType.MESH
NS = 16
DTR = 48
KC = 4
BLK = 128
NBF = 32
DI = 1536
D = 768
TOK = 256
CH = 96
LANES = 128
TILES = DI // LANES
CHUNKS = 8
STEPS = TOK // CHUNKS
WROWS = 24
TROWS = 48
WB = DTR + DTR + 2 * NS
SEATS = 8
VMEM_LIMIT = 56 * 1024 * 1024
LOG2E = 1.4426950408889634
F32 = jnp.float32
BF16 = jnp.bfloat16


def scan_rows():
    r = lax.broadcasted_iota(jnp.int32, (TOK, TOK), 0)
    i = lax.broadcasted_iota(jnp.int32, (TOK, TOK), 1)
    return ((r & (CHUNKS - 1)) * STEPS + (r >> 3) == i).astype(F32).astype(BF16)


def token_rows():
    i = lax.broadcasted_iota(jnp.int32, (TOK, TOK), 0)
    r = lax.broadcasted_iota(jnp.int32, (TOK, TOK), 1)
    return ((r & (CHUNKS - 1)) * STEPS + (r >> 3) == i).astype(F32).astype(BF16)


def silu(v):
    half = 0.5 * v
    return half + half * jnp.tanh(half)


def lanes_of(tile, width=LANES):
    return pl.ds(pl.multiple_of(tile * width, width), width)


def spread_columns(projected, first, out):
    for n in range(NS):
        out[n] = jnp.broadcast_to(projected[:, first + n : first + n + 1], (TOK, LANES))


def layer(
    x, z, cw, cb, pwt, sw, sb, dl, sg, order, out,
    xv, zv, gwf, gwb, gt, tstage, tsend, trecv, where_to,
    wfa, wba, xf, sigt, gz, signal, step, rate2, rate_own, in_b, out_b, inner, reach, y, gated, grown,
    sends, recv, scan_e, scan_t, pk1, got1, pk2, got2, bsend, back, fsend, fback,
    local, s1, r1, s2, r2, st, rt, sa, ra, sb1, rb1, sc, rc, sd, rd, sf, rf, up, down,
):
    f = lax.axis_index("tm")
    s = lax.axis_index("space")
    frames = lax.axis_size("tm")
    width = lax.axis_size("space")
    outer = frames // SEATS
    row = s // 4
    side = s // 2 % 2
    core = s % 2
    part = f // SEATS
    seat = f % SEATS
    sibling = (f, s - core + 1 - core)
    twin = f + 1 - f % 2 * 2
    ahead = ((f + 1) % frames, s)
    behind = ((f + frames - 1) % frames, s)
    full = (CHUNKS, LANES)
    slot = (3, CHUNKS, LANES)
    sub = lax.broadcasted_iota(jnp.int32, full, 0)
    sub3 = lax.broadcasted_iota(jnp.int32, slot, 1)
    zero = jnp.zeros(full, F32)

    def chip(dx, dy):
        return (row + dx) % 4 * 4 + (side + dy) % 2 * 2 + core

    def near(d):
        return part * SEATS + (seat + d) % SEATS

    def far(d):
        return ((part + d) % outer) * SEATS + seat

    def remote(src, dst, ssem, rsem, target):
        return pltpu.make_async_remote_copy(
            src_ref=src,
            dst_ref=dst,
            send_sem=ssem,
            recv_sem=rsem,
            device_id=target,
            device_id_type=MESH,
        )

    def push(src, dst, ssem, rsem, target):
        copy = remote(src, dst, ssem, rsem, target)
        copy.start()
        return copy

    load_x = pltpu.make_async_copy(x, xv, local.at[0])
    load_z = pltpu.make_async_copy(z, zv, local.at[1])
    load_x.start()

    barrier = pltpu.get_barrier_semaphore()
    for d in range(1, width):
        pl.semaphore_signal(barrier, inc=1, device_id=(f, (s + d) % width), device_id_type=MESH)
    for d in range(1, SEATS):
        pl.semaphore_signal(barrier, inc=1, device_id=(near(d), s), device_id_type=MESH)
    above = ((f + 2) % frames, s)
    below = ((f + frames - 2) % frames, s)
    for neighbour in (above, below):
        pl.semaphore_signal(barrier, inc=1, device_id=neighbour, device_id_type=MESH)
    pl.semaphore_signal(barrier, inc=1, device_id=behind, device_id_type=MESH)
    for dx in range(4):
        pl.semaphore_signal(barrier, inc=1, device_id=(twin, chip(dx, 1)), device_id_type=MESH)

    load_z.start()
    gwf[s, 0:KC] = cw[...]
    gwf[s, KC : KC + 1] = cb[...]
    gwf[s, 5:6] = sb[...]
    gwf[s, 6:7] = sg[...]
    gwf[s, 7:8] = jnp.zeros((1, CH), F32)
    gwf[s, 8:WROWS] = dl[...]
    gwb[s, 0:DTR] = sw[...]
    gwb[s, DTR:WB] = pwt[...]
    tstage[...] = jnp.zeros_like(tstage)
    load_x.wait()
    for b in range(2):
        ends = xv[BLK * (b + 1) - 16 : BLK * (b + 1)].astype(F32)
        for t in range(KC - 1):
            for j in range(TILES):
                line = ends[13 + t : 14 + t, LANES * j : LANES * (j + 1)]
                tstage[b, t * TILES + j : t * TILES + j + 1] = line
    gt[pl.ds(2 * s, 2)] = tstage[...].astype(BF16)
    pl.semaphore_wait(barrier, width + SEATS + 5)

    def place(a, i):
        return (gwf.at[i], gt.at[pl.ds(2 * i, 2)], gwb.at[i])[a]

    sent = []
    relayed = [0, 0, 0]

    def relay(a, dx, dy, tx, ty):
        ref = place(a, chip(dx, dy))
        landing = (dx - tx) % 4 * 2 + (dy - ty) % 2
        ssem = s1.at[a, relayed[a]]
        relayed[a] += 1
        frame = twin if ty and a != 1 else f
        sent.append(push(ref, ref, ssem, r1.at[a, landing], (frame, chip(tx, ty))))

    def share(a, dx, dy):
        ref = place(a, chip(dx, dy))
        k = dx * 2 + dy
        sent.append(push(ref, ref, s2.at[a, k], r2.at[a, k], sibling))

    def take(a, dx, dy):
        ref = place(a, chip(dx, dy))
        remote(ref, ref, s1.at[a, 0], r1.at[a, dx * 2 + dy], sibling).wait_recv()

    def offer(a):
        for tx, ty in ((1, 0), (3, 0), (0, 1), (1, 1), (3, 1), (2, 0), (2, 1)):
            relay(a, 0, 0, tx, ty)
        share(a, 0, 0)

    def collect(a):
        for dx, dy in ((3, 0), (1, 0), (0, 1), (3, 1), (1, 1), (2, 0), (2, 1)):
            take(a, dx, dy)
            share(a, dx, dy)

    def own_item(a):
        for tx, ty in ((1, 0), (3, 0), (0, 1), (1, 1), (3, 1)):
            relay(a, 0, 0, tx, ty)
        share(a, 0, 0)

    def neighbours(a):
        for dy in range(2):
            take(a, 1, dy)
            relay(a, 1, dy, 3, 0)
            share(a, 1, dy)
        for dx, dy in ((3, 0), (0, 1), (3, 1)):
            take(a, dx, dy)
            share(a, dx, dy)

    def opposite(a):
        for dy in range(2):
            take(a, 2, dy)
            share(a, 2, dy)

    def from_sibling(a):
        for dx in range(4):
            for dy in range(2):
                ref = place(a, chip(dx, dy) - core + 1 - core)
                k = dx * 2 + dy
                remote(ref, ref, s2.at[a, k], r2.at[a, k], sibling).wait_recv()

    passed_on = [0]

    def pass_ready():
        k = passed_on[0]
        if 0 < k <= 7:
            pl.semaphore_wait(up, 1)
        if 0 < k <= 3:
            pl.semaphore_wait(down, 1)
        if k < 7:
            pl.semaphore_signal(up, inc=1, device_id=below, device_id_type=MESH)
        if k < 3:
            pl.semaphore_signal(down, inc=1, device_id=above, device_id_type=MESH)
        passed_on[0] += 1

    offer(0)
    offer(1)
    own_item(2)
    pass_ready()
    listed = [order[j] for j in range(NBF)]

    def inverse(r, carry):
        found = 0
        for j in range(NBF):
            found = jnp.where(listed[j] == r, j, found)
        where_to[r] = found
        return carry

    lax.fori_loop(0, NBF, inverse, 0)
    for b in range(2):
        xf[b, 0:8] = jnp.zeros((8, DI), F32)

    def widen(tile, carry):
        lanes = lanes_of(tile)
        for b in range(2):
            xf[b, 8 : 8 + BLK, lanes] = xv[BLK * b : BLK * (b + 1), lanes].astype(F32)
        return carry

    lax.fori_loop(0, TILES, widen, 0)
    sends[...] = jnp.zeros_like(sends)
    collect(0)
    pass_ready()
    collect(1)
    pass_ready()
    neighbours(2)
    from_sibling(0)
    for i in range(DI // CH):
        wfa[:, CH * i : CH * (i + 1)] = gwf[i]

    def filtered(b, count, lanes):
        total = wfa[4:5, lanes]
        for k in range(KC):
            total = total + wfa[k : k + 1, lanes] * xf[b, 5 + k : 5 + k + count, lanes]
        return silu(total).astype(BF16)

    def convolve(tile, carry):
        lanes = lanes_of(tile)
        for b in range(2):
            sigt[BLK * b : BLK * (b + 1), lanes] = filtered(b, BLK, lanes)
        return carry

    lax.fori_loop(0, 3, convolve, 0)
    pass_ready()
    opposite(2)
    from_sibling(1)
    tsend[...] = gt[order[NBF - 1]]
    sent_tail = push(tsend, trecv, st, rt, ahead)
    sent.append(sent_tail)
    lax.fori_loop(3, TILES, convolve, 0)
    pass_ready()
    rate2[...] = -jnp.exp(wfa[8:WROWS]) * LOG2E
    rearranged = scan_rows()
    load_z.wait()

    def gate(chunk, carry):
        lanes = lanes_of(chunk, 256)
        zs = jnp.dot(rearranged, zv[:, lanes], preferred_element_type=F32)
        gz[:, lanes] = silu(zs)
        return carry

    lax.fori_loop(0, DI // 256, gate, 0)
    pass_ready()
    from_sibling(2)
    for i in range(DI // CH):
        wba[:, CH * i : CH * (i + 1)] = gwb[i].astype(F32)
    sent_tail.wait_recv()
    came = trecv[...].astype(F32)
    opening = jnp.full(came.shape, f, jnp.int32) == 0
    gt[NBF] = jnp.where(opening, 0.0, came).astype(BF16)
    for b in range(2):
        at = where_to[2 * s + b]
        before = jnp.where(at == 0, NBF, order[jnp.maximum(at - 1, 0)])
        halo = gt[before].astype(F32)
        for t in range(KC - 1):
            for j in range(TILES):
                line = halo[t * TILES + j : t * TILES + j + 1]
                xf[b, 5 + t : 6 + t, LANES * j : LANES * (j + 1)] = line

    def heads(tile, carry):
        lanes = lanes_of(tile)
        for b in range(2):
            sigt[BLK * b : BLK * b + 16, lanes] = filtered(b, 16, lanes)
        return carry

    lax.fori_loop(0, TILES, heads, 0)

    def rearrange(chunk, carry):
        lanes = lanes_of(chunk, 256)
        signal[:, lanes] = jnp.dot(rearranged, sigt[:, lanes], preferred_element_type=F32)
        return carry

    lax.fori_loop(0, DI // 256, rearrange, 0)
    pass_ready()
    proj = lax.dot_general(
        signal[...].astype(BF16),
        wba[DTR:WB].astype(BF16),
        (((1,), (1,)), ((), ())),
        preferred_element_type=F32,
    )
    spread_columns(proj, DTR, in_b)
    rank = proj[:, :DTR]
    high = rank.astype(BF16)
    rest = rank - high.astype(F32)
    mid = rest.astype(BF16)
    low = (rest - mid.astype(F32)).astype(BF16)

    def steps(chunk, carry):
        lanes = lanes_of(chunk, 256)
        weight = wba[0:DTR, lanes].astype(BF16)
        total = wfa[5:6, lanes] + jnp.dot(low, weight, preferred_element_type=F32)
        total = total + jnp.dot(mid, weight, preferred_element_type=F32)
        total = total + jnp.dot(high, weight, preferred_element_type=F32)
        step[:, lanes] = jnp.maximum(total, 0.0) + jnp.log1p(jnp.exp(-jnp.abs(total)))
        return carry

    lax.fori_loop(0, DI // 256, steps, 0)
    pass_ready()
    m1 = sub % 4 >= 1
    m2 = sub % 4 >= 2

    def rows_of(t):
        return pl.ds(pl.multiple_of(t * CHUNKS, CHUNKS), CHUNKS)

    def rates_of(lanes):
        return [jnp.broadcast_to(rate2[n : n + 1, lanes], full) for n in range(NS)]

    def block_states(tile, carry):
        lanes = lanes_of(tile)
        rates = rates_of(lanes)

        def one(t, held):
            states, total = held
            rows = rows_of(t)
            now = step[rows, lanes]
            drive = now * signal[rows, lanes]
            decay = [jnp.exp2(now * rates[n]) for n in range(NS)]
            for n in range(NS):
                grown[n, rows, lanes] = decay[n]
            states = tuple(decay[n] * states[n] + in_b[n, rows, :] * drive for n in range(NS))
            return states, total + now

        states, total = lax.fori_loop(0, STEPS, one, ((zero,) * NS, zero), unroll=4)
        sum1 = total + jnp.where(m1, pltpu.roll(total, 1, 0), 0.0)
        sum2 = sum1 + jnp.where(m2, pltpu.roll(sum1, 2, 0), 0.0)
        reach[:, lanes] = jnp.where(m1, pltpu.roll(sum2, 1, 0), 0.0)
        ends = jnp.where(
            sub < 4, jnp.broadcast_to(sum2[3:4], full), jnp.broadcast_to(sum2[7:8], full)
        )
        group = tile // 3
        place = tile % 3
        for h in range(4):
            state_out = zero
            rate_out = zero
            for q in range(4):
                n = 4 * h + q
                decay = jnp.exp2(rates[n] * total)
                one_s = states[n] + jnp.where(m1, decay * pltpu.roll(states[n], 1, 0), 0.0)
                decay2 = jnp.exp2(rates[n] * sum1)
                two_s = one_s + jnp.where(m2, decay2 * pltpu.roll(one_s, 2, 0), 0.0)
                inner[n, :, lanes] = jnp.where(m1, pltpu.roll(two_s, 1, 0), 0.0)
                turn = (q + 5) % 8
                moved = pltpu.roll(two_s, turn, 0) if turn else two_s
                state_out = jnp.where(sub % 4 == q, moved, state_out)
                rate_out = jnp.where(sub % 4 == q, rates[n], rate_out)
            sends[group * 4 + h, place] = state_out
            sends[group * 4 + h, 3] = jnp.where(sub % 4 == place, ends, sends[group * 4 + h, 3])
            rate_own[h, tile] = rate_out
        return carry

    def to_owner(peer):
        return remote(sends.at[peer], recv.at[s], sa.at[peer], ra.at[s], (f, peer))

    def one_group(g, carry):
        lax.fori_loop(g * 3, g * 3 + 3, block_states, 0)
        for h in range(4):
            peer = g * 4 + h

            @pl.when(peer != s)
            def _():
                to_owner(peer).start()

        return carry

    lax.fori_loop(0, 4, one_group, 0)
    recv[s] = sends[s]
    spread_columns(proj, DTR + NS, out_b)

    def own_outputs(tile, carry):
        lanes = lanes_of(tile)
        rates = rates_of(lanes)
        skip = jnp.broadcast_to(wfa[6:7, lanes], full)

        def one(t, held):
            states, reached = held
            rows = rows_of(t)
            sig = signal[rows, lanes]
            drive = step[rows, lanes] * sig
            decay = [grown[n, rows, lanes] for n in range(NS)]
            states = tuple(decay[n] * states[n] + in_b[n, rows, :] * drive for n in range(NS))
            reached = tuple(decay[n] * reached[n] for n in range(NS))
            coeffs = [out_b[n, rows, :] for n in range(NS)]
            terms = [coeffs[n] * states[n] for n in range(NS)]
            for n in range(NS):
                grown[n, rows, lanes] = coeffs[n] * reached[n]
            while len(terms) > 1:
                terms = [a + b for a, b in zip(terms[::2], terms[1::2])]
            y[rows, lanes] = terms[0] + skip * sig
            return states, reached

        states = tuple(inner[n, :, lanes] for n in range(NS))
        reached = tuple(jnp.exp2(rates[n] * reach[:, lanes]) for n in range(NS))
        lax.fori_loop(0, STEPS, one, (states, reached), unroll=2)
        return carry

    lax.fori_loop(0, 3, own_outputs, 0)
    for d in range(1, width):
        peer = (s + d) % width
        remote(sends.at[peer], recv.at[peer], sa.at[peer], ra.at[peer], (f, peer)).wait_recv()

    def turned(v):
        return pltpu.roll(v, 4, len(v.shape) - 2)

    my_group = s // 4
    my_rates = rate_own[s % 4, pl.ds(my_group * 3, 3)]

    def decays(sums):
        spread = [jnp.broadcast_to(sums[i : i + 1], full) for i in range(3)]
        return jnp.exp2(my_rates * jnp.stack(spread))

    def through(j, carry):
        e, passed = carry
        scan_e[j] = e
        scan_t[j] = passed
        block = order[j]
        got = recv[lax.shift_right_logical(block, 1)]
        odd = jnp.full((4, CHUNKS, LANES), block & 1, jnp.int32) == 1
        got = jnp.where(odd, turned(got), got)
        return decays(got[3]) * e + got[0:3], passed + got[3]

    zero3 = jnp.zeros(slot, F32)
    unit3 = jnp.ones(slot, F32)
    e, passed = lax.fori_loop(0, NBF, through, (zero3, zero), unroll=8)
    p = decays(passed)
    pk1[...] = jnp.where(sub3 < 4, p, turned(e))
    got1[seat] = pk1[...]
    level1 = []
    for d in range(1, SEATS):
        level1.append(push(pk1, got1.at[seat], sb1.at[d], rb1.at[d], (near(d), s)))

    def pack(d, carry):
        i0 = where_to[2 * d]
        i1 = where_to[2 * d + 1]
        bsend[d, 0:3] = jnp.where(sub3 < 4, scan_e[i0], turned(scan_e[i1]))
        bsend[d, 3] = jnp.where(sub < 4, scan_t[i0], turned(scan_t[i1]))
        return carry

    lax.fori_loop(0, width, pack, 0, unroll=4)
    back[s] = bsend[s]
    returns = []
    for d in range(1, width):
        peer = (s + d) % width
        returns.append(push(bsend.at[peer], back.at[s], sd.at[peer], rd.at[s], (f, peer)))
    lax.fori_loop(3, 6, own_outputs, 0)
    for copy in level1:
        copy.wait_recv()

    def gather_near(m, carry):
        e_in, p_in, e_all, p_all = carry
        got = got1[m]
        moved = turned(got)
        early = jnp.full(slot, m, jnp.int32) < jnp.full(slot, seat, jnp.int32)
        e_in = jnp.where(early, got * e_in + moved, e_in)
        p_in = jnp.where(early, got * p_in, p_in)
        return e_in, p_in, got * e_all + moved, got * p_all

    begin = (zero3, unit3, zero3, unit3)
    e_in, p_in, e_all, p_all = lax.fori_loop(0, SEATS, gather_near, begin, unroll=SEATS)
    pk2[...] = jnp.where(sub3 < 4, p_all, turned(e_all))
    got2[part] = pk2[...]
    level2 = []
    for d in range(1, outer):
        level2.append(push(pk2, got2.at[part], sc.at[d], rc.at[d], (far(d), s)))
    lax.fori_loop(6, 9, own_outputs, 0)
    for copy in level2:
        copy.wait_recv()

    def gather_far(m, start):
        got = got2[m]
        early = jnp.full(slot, m, jnp.int32) < jnp.full(slot, part, jnp.int32)
        return jnp.where(early, got * start + turned(got), start)

    start = lax.fori_loop(0, outer, gather_far, zero3, unroll=4)
    start = p_in * start + e_in

    first = jnp.where(sub < 4, start[0], turned(start[1]))
    fsend[...] = jnp.concatenate([first, start[2]], axis=0).astype(BF16)
    fback[s] = fsend[...]
    starts = []
    for d in range(1, width):
        peer = (s + d) % width
        starts.append(push(fsend, fback.at[s], sf.at[peer], rf.at[s], (f, peer)))
    lax.fori_loop(9, 12, own_outputs, 0)
    for d in range(1, width):
        peer = (s + d) % width
        remote(bsend.at[peer], back.at[peer], sd.at[peer], rd.at[peer], (f, peer)).wait_recv()

    def both(tile8, r):
        return jnp.where(
            sub < 4,
            jnp.broadcast_to(tile8[r : r + 1], full),
            jnp.broadcast_to(tile8[4 + r : 5 + r], full),
        )

    def complete(g, place):
        lanes = lanes_of(g * 3 + place)
        rates = rates_of(lanes)
        passed = both(back[g * 4, 3], place)
        entering = []
        for h in range(4):
            came = back[g * 4 + h, place]
            begun = fback[g * 4 + h].astype(F32)
            for q in range(4):
                r = place * 4 + q
                line = jnp.broadcast_to(begun[r : r + 1], full)
                entering.append(both(came, q) + jnp.exp2(rates[4 * h + q] * passed) * line)

        def one(t, carry):
            rows = rows_of(t)
            terms = [grown[n, rows, lanes] * entering[n] for n in range(NS)]
            while len(terms) > 1:
                terms = [a + b for a, b in zip(terms[::2], terms[1::2])]
            scanned = (y[rows, lanes] + terms[0]).astype(BF16).astype(F32)
            y[rows, lanes] = scanned * gz[rows, lanes]
            return carry

        lax.fori_loop(0, STEPS, one, 0, unroll=4)
        gated[:, lanes] = y[:, lanes].astype(BF16)

    undo = token_rows()

    def one_group_back(g, carry):
        for h in range(4):
            peer = g * 4 + h

            @pl.when(peer != s)
            def _():
                remote(fsend, fback.at[peer], sf.at[peer], rf.at[peer], (f, peer)).wait_recv()

        for place in range(3):
            complete(g, place)
        lanes = lanes_of(g, 3 * LANES)
        out[:, lanes] = jnp.dot(undo, gated[:, lanes], preferred_element_type=F32).astype(BF16)
        return carry

    lax.fori_loop(0, 4, one_group_back, 0)
    for copy in sent + level1 + level2 + returns + starts:
        copy.wait_send()
    for d in range(1, width):
        to_owner((s + d) % width).wait_send()


def shards(
    inner_x,
    inner_z,
    conv_weight,
    conv_bias,
    proj_weight,
    step_weight,
    step_bias,
    decay_log,
    skip_gain,
    out_weight,
    order_table,
):
    frames, rows, columns, channels = inner_x.shape
    space = lax.axis_size("space")
    outer = lax.axis_size("tm") // SEATS
    dma = pltpu.SemaphoreType.DMA
    slot = (3, CHUNKS, LANES)
    anyw = pl.BlockSpec(memory_space=pl.ANY)
    vm = pl.BlockSpec(memory_space=pltpu.VMEM)
    held = [
        ((TOK, DI), BF16),
        ((TOK, DI), BF16),
        ((space, WROWS, CH), F32),
        ((space, WB, CH), BF16),
        ((NBF + 1, TROWS, LANES), BF16),
        ((2, TROWS, LANES), F32),
        ((TROWS, LANES), BF16),
        ((TROWS, LANES), BF16),
        None,
        ((WROWS, DI), F32),
        ((WB, DI), F32),
        ((2, BLK + 8, DI), F32),
        ((TOK, DI), BF16),
        ((TOK, DI), F32),
        ((TOK, DI), F32),
        ((TOK, DI), F32),
        ((NS, DI), F32),
        ((4, TILES, CHUNKS, LANES), F32),
        ((NS, TOK, LANES), F32),
        ((NS, TOK, LANES), F32),
        ((NS, CHUNKS, DI), F32),
        ((CHUNKS, DI), F32),
        ((TOK, DI), F32),
        ((TOK, DI), BF16),
        ((NS, TOK, DI), F32),
        ((space, 4, CHUNKS, LANES), F32),
        ((space, 4, CHUNKS, LANES), F32),
        ((NBF,) + slot, F32),
        ((NBF, CHUNKS, LANES), F32),
        (slot, F32),
        ((SEATS,) + slot, F32),
        (slot, F32),
        ((outer,) + slot, F32),
        ((space, 4, CHUNKS, LANES), F32),
        ((space, 4, CHUNKS, LANES), F32),
        ((16, LANES), BF16),
        ((space, 16, LANES), BF16),
    ]
    scratch = [pltpu.SMEM((NBF,), jnp.int32) if h is None else pltpu.VMEM(*h) for h in held]
    scratch += [dma((2,))] + [dma((3, 8))] * 4 + [dma] * 2
    scratch += [dma((16,))] * 2 + [dma((8,))] * 4 + [dma((16,))] * 4
    scratch += [pltpu.SemaphoreType.REGULAR] * 2
    gated = pl.pallas_call(
        layer,
        out_shape=jax.ShapeDtypeStruct((TOK, DI), BF16),
        in_specs=[anyw, anyw] + [vm] * 7 + [pl.BlockSpec(memory_space=pltpu.SMEM)],
        out_specs=vm,
        scratch_shapes=scratch,
        compiler_params=pltpu.CompilerParams(
            collective_id=0, has_side_effects=True, vmem_limit_bytes=VMEM_LIMIT
        ),
        name="layer",
    )(
        inner_x.reshape(TOK, DI),
        inner_z.reshape(TOK, DI),
        conv_weight,
        conv_bias.reshape(1, CH),
        proj_weight.T,
        step_weight,
        step_bias.reshape(1, CH),
        decay_log,
        skip_gain.reshape(1, CH),
        order_table,
    )
    mixed = jnp.dot(gated, out_weight, preferred_element_type=F32).astype(BF16)
    return mixed.reshape(frames, rows, columns, D)


def solution(mesh):
    in_specs = (
        P("tm", "space", None, None),
        P("tm", "space", None, None),
        P(None, "space"),
        P("space"),
        P("space", None),
        P(None, "space"),
        P("space"),
        P(None, "space"),
        P("space"),
        P(),
        P(),
    )
    out_specs = P("tm", "space", None, None)
    return jax.shard_map(shards, mesh=mesh, in_specs=in_specs, out_specs=out_specs, check_vma=False)
```

```python
import jax
import jax.numpy as jnp
from jax import lax
from jax.experimental import pallas as pl
from jax.experimental.pallas import tpu as pltpu
from jax.sharding import PartitionSpec as P

MESH = pl.DeviceIdType.MESH
NS = 16
DTR = 48
KC = 4
BLK = 128
NBF = 32
DI = 1536
D = 768
TOK = 256
CH = 96
LANES = 128
TILES = DI // LANES
CHUNKS = 8
STEPS = TOK // CHUNKS
WROWS = 24
TROWS = 48
TAIL = (KC - 1) * TILES
PAIR = 80
WB = DTR + DTR + 2 * NS
SEATS = 8
VMEM_LIMIT = 56 * 1024 * 1024
LOG2E = 1.4426950408889634
F32 = jnp.float32
BF16 = jnp.bfloat16


def scan_rows():
    r = lax.broadcasted_iota(jnp.int32, (TOK, TOK), 0)
    i = lax.broadcasted_iota(jnp.int32, (TOK, TOK), 1)
    return ((r & (CHUNKS - 1)) * STEPS + (r >> 3) == i).astype(F32).astype(BF16)


def token_rows():
    i = lax.broadcasted_iota(jnp.int32, (TOK, TOK), 0)
    r = lax.broadcasted_iota(jnp.int32, (TOK, TOK), 1)
    return ((r & (CHUNKS - 1)) * STEPS + (r >> 3) == i).astype(F32).astype(BF16)


def silu(v):
    half = 0.5 * v
    return half + half * jnp.tanh(half)


def lanes_of(tile, width=LANES):
    return pl.ds(pl.multiple_of(tile * width, width), width)


def spread_columns(projected, first, out):
    for n in range(NS):
        out[n] = jnp.broadcast_to(projected[:, first + n : first + n + 1], (TOK, LANES))


def layer(
    x, z, cw, cb, pwt, sw, sb, dl, sg, order, out,
    xv, zv, gwf, gwb, gt, tstage, wstage, tsel, tsend, trecv, where_to,
    wfa, wba, xf, sigt, gz, signal, step, rate2, rate_own, in_b, out_b, inner, reach, y, gated, grown,
    sends, recv, scan_e, scan_t, pk1, got1, pk2, got2, bsend, back, fsend, fback,
    local, s1, r1, s2, r2, st, rt, sa, ra, sb1, rb1, sc, rc, sd, rd, sf, rf,
):
    f = lax.axis_index("tm")
    s = lax.axis_index("space")
    frames = lax.axis_size("tm")
    width = lax.axis_size("space")
    outer = frames // SEATS
    row = s // 4
    side = s // 2 % 2
    core = s % 2
    part = f // SEATS
    seat = f % SEATS
    sibling = (f, s - core + 1 - core)
    twin = f + 1 - f % 2 * 2
    ahead = ((f + 1) % frames, s)
    behind = ((f + frames - 1) % frames, s)
    full = (CHUNKS, LANES)
    slot = (3, CHUNKS, LANES)
    sub = lax.broadcasted_iota(jnp.int32, full, 0)
    sub3 = lax.broadcasted_iota(jnp.int32, slot, 1)
    zero = jnp.zeros(full, F32)

    def chip(dx, dy):
        return (row + dx) % 4 * 4 + (side + dy) % 2 * 2 + core

    def near(d):
        return part * SEATS + (seat + d) % SEATS

    def far(d):
        return ((part + d) % outer) * SEATS + seat

    def remote(src, dst, ssem, rsem, target):
        return pltpu.make_async_remote_copy(
            src_ref=src,
            dst_ref=dst,
            send_sem=ssem,
            recv_sem=rsem,
            device_id=target,
            device_id_type=MESH,
        )

    def push(src, dst, ssem, rsem, target):
        copy = remote(src, dst, ssem, rsem, target)
        copy.start()
        return copy

    load_x = pltpu.make_async_copy(x, xv, local.at[0])
    load_z = pltpu.make_async_copy(z, zv, local.at[1])
    load_x.start()

    barrier = pltpu.get_barrier_semaphore()
    for d in range(1, width):
        pl.semaphore_signal(barrier, inc=1, device_id=(f, (s + d) % width), device_id_type=MESH)
    for d in range(1, SEATS):
        pl.semaphore_signal(barrier, inc=1, device_id=(near(d), s), device_id_type=MESH)
    for d in range(1, outer):
        pl.semaphore_signal(barrier, inc=1, device_id=(far(d), s), device_id_type=MESH)
    pl.semaphore_signal(barrier, inc=1, device_id=behind, device_id_type=MESH)
    for dx in range(4):
        pl.semaphore_signal(barrier, inc=1, device_id=(twin, chip(dx, 1)), device_id_type=MESH)

    load_z.start()
    gwf[s, 0:KC] = cw[...]
    gwf[s, KC : KC + 1] = cb[...]
    gwf[s, 5:6] = sb[...]
    gwf[s, 6:7] = sg[...]
    gwf[s, 7:8] = jnp.zeros((1, CH), F32)
    gwf[s, 8:WROWS] = dl[...]
    narrow = pwt[...].astype(F32)
    wstage[0:DTR, 0:CH] = sw[...].astype(F32)
    wstage[DTR:CH, 0:CH] = narrow[0:DTR]
    for m in range(3):
        wstage[32 * m : 32 * (m + 1), CH:LANES] = narrow[DTR:, 32 * m : 32 * (m + 1)]
    gwb[s] = wstage[...].astype(BF16)
    tstage[...] = jnp.zeros_like(tstage)
    load_x.wait()
    for b in range(2):
        ends = xv[BLK * (b + 1) - 16 : BLK * (b + 1)].astype(F32)
        for t in range(KC - 1):
            for j in range(TILES):
                line = ends[13 + t : 14 + t, LANES * j : LANES * (j + 1)]
                at = b * TAIL + t * TILES + j
                tstage[at : at + 1] = line
    gt[s] = tstage[...].astype(BF16)
    pl.semaphore_wait(barrier, width + SEATS + outer + 2)

    def place(a, i):
        return (gwf.at[i], gt.at[i], gwb.at[i])[a]

    sent = []
    relayed = [0, 0, 0]

    def relay(a, dx, dy, tx, ty):
        ref = place(a, chip(dx, dy))
        landing = (dx - tx) % 4 * 2 + (dy - ty) % 2
        ssem = s1.at[a, relayed[a]]
        relayed[a] += 1
        frame = twin if ty and a != 1 else f
        sent.append(push(ref, ref, ssem, r1.at[a, landing], (frame, chip(tx, ty))))

    def tail_of(block):
        pair = gt[lax.shift_right_logical(block, 1)].astype(F32)
        odd = jnp.full((TAIL, LANES), block & 1, jnp.int32) == 1
        return jnp.where(odd, pair[TAIL : 2 * TAIL], pair[0:TAIL])

    def share(a, dx, dy):
        ref = place(a, chip(dx, dy))
        k = dx * 2 + dy
        sent.append(push(ref, ref, s2.at[a, k], r2.at[a, k], sibling))

    def take(a, dx, dy):
        ref = place(a, chip(dx, dy))
        remote(ref, ref, s1.at[a, 0], r1.at[a, dx * 2 + dy], sibling).wait_recv()

    def offer(a, targets):
        for tx, ty in targets:
            relay(a, 0, 0, tx, ty)
        share(a, 0, 0)

    def collect(a, items):
        for dx, dy in items:
            take(a, dx, dy)
            share(a, dx, dy)

    def other_side(a):
        take(a, 0, 1)
        relay(a, 0, 1, 1, 0)
        relay(a, 0, 1, 3, 0)
        if a == 1:
            relay(a, 0, 1, 2, 0)
        share(a, 0, 1)

    def neighbours(a):
        for dy in range(2):
            take(a, 1, dy)
            relay(a, 1, dy, 3, 0)
            share(a, 1, dy)
        for dy in range(2):
            take(a, 3, dy)
            share(a, 3, dy)

    def opposite(a):
        for dy in range(2):
            take(a, 2, dy)
            share(a, 2, dy)

    def from_sibling(a):
        for dx in range(4):
            for dy in range(2):
                ref = place(a, chip(dx, dy) - core + 1 - core)
                k = dx * 2 + dy
                remote(ref, ref, s2.at[a, k], r2.at[a, k], sibling).wait_recv()

    offer(0, ((0, 1), (1, 1), (3, 1), (2, 1), (1, 0), (3, 0), (2, 0)))
    offer(1, ((0, 1), (2, 0), (1, 0), (3, 0)))
    offer(2, ((0, 1), (1, 0), (3, 0)))
    listed = [order[j] for j in range(NBF)]

    def inverse(r, carry):
        found = 0
        for j in range(NBF):
            found = jnp.where(listed[j] == r, j, found)
        where_to[r] = found
        return carry

    lax.fori_loop(0, NBF, inverse, 0)
    for b in range(2):
        xf[b, 0:8] = jnp.zeros((8, DI), F32)

    def widen(tile, carry):
        lanes = lanes_of(tile)
        for b in range(2):
            xf[b, 8 : 8 + BLK, lanes] = xv[BLK * b : BLK * (b + 1), lanes].astype(F32)
        return carry

    lax.fori_loop(0, TILES, widen, 0)
    sends[...] = jnp.zeros_like(sends)
    other_side(1)
    other_side(2)
    collect(0, ((3, 0), (1, 0), (0, 1), (3, 1), (1, 1), (2, 0), (2, 1)))
    collect(1, ((1, 0), (3, 0), (2, 0), (1, 1), (3, 1), (2, 1)))
    from_sibling(0)
    for i in range(DI // CH):
        wfa[:, CH * i : CH * (i + 1)] = gwf[i]

    def filtered(b, count, lanes):
        total = wfa[4:5, lanes]
        for k in range(KC):
            total = total + wfa[k : k + 1, lanes] * xf[b, 5 + k : 5 + k + count, lanes]
        return silu(total).astype(BF16)

    def convolve(tile, carry):
        lanes = lanes_of(tile)
        for b in range(2):
            sigt[BLK * b : BLK * (b + 1), lanes] = filtered(b, BLK, lanes)
        return carry

    lax.fori_loop(0, 3, convolve, 0)
    neighbours(2)
    lax.fori_loop(3, 6, convolve, 0)
    from_sibling(1)
    tsel[...] = jnp.zeros_like(tsel)
    tsel[0:TAIL] = tail_of(order[NBF - 1])
    tsend[...] = tsel[...].astype(BF16)
    sent_tail = push(tsend, trecv, st, rt, ahead)
    sent.append(sent_tail)
    opposite(2)
    lax.fori_loop(6, TILES, convolve, 0)
    rate2[...] = -jnp.exp(wfa[8:WROWS]) * LOG2E
    rearranged = scan_rows()
    load_z.wait()

    def gate(chunk, carry):
        lanes = lanes_of(chunk, 256)
        zs = jnp.dot(rearranged, zv[:, lanes], preferred_element_type=F32)
        gz[:, lanes] = silu(zs)
        return carry

    lax.fori_loop(0, DI // 256, gate, 0)
    from_sibling(2)
    for i in range(DI // CH):
        held = gwb[i].astype(F32)
        wba[0:CH, CH * i : CH * (i + 1)] = held[:, 0:CH]
        for m in range(3):
            at = CH * i + 32 * m
            wba[CH:WB, at : at + 32] = held[32 * m : 32 * (m + 1), CH:LANES]
    sent_tail.wait_recv()
    came = trecv[...].astype(F32)[0:TAIL]
    came = jnp.where(jnp.full(came.shape, f, jnp.int32) == 0, 0.0, came)
    for b in range(2):
        at = where_to[2 * s + b]
        found = tail_of(order[jnp.maximum(at - 1, 0)])
        halo = jnp.where(jnp.full(came.shape, at, jnp.int32) == 0, came, found)
        for t in range(KC - 1):
            for j in range(TILES):
                line = halo[t * TILES + j : t * TILES + j + 1]
                xf[b, 5 + t : 6 + t, LANES * j : LANES * (j + 1)] = line

    def heads(tile, carry):
        lanes = lanes_of(tile)
        for b in range(2):
            sigt[BLK * b : BLK * b + 16, lanes] = filtered(b, 16, lanes)
        return carry

    lax.fori_loop(0, TILES, heads, 0)

    def rearrange(chunk, carry):
        lanes = lanes_of(chunk, 256)
        signal[:, lanes] = jnp.dot(rearranged, sigt[:, lanes], preferred_element_type=F32)
        return carry

    lax.fori_loop(0, DI // 256, rearrange, 0)
    proj = lax.dot_general(
        signal[...].astype(BF16),
        wba[DTR:WB].astype(BF16),
        (((1,), (1,)), ((), ())),
        preferred_element_type=F32,
    )
    spread_columns(proj, DTR, in_b)
    rank = proj[:, :DTR]
    high = rank.astype(BF16)
    low = (rank - high.astype(F32)).astype(BF16)

    def steps(chunk, carry):
        lanes = lanes_of(chunk, 256)
        weight = wba[0:DTR, lanes].astype(BF16)
        total = wfa[5:6, lanes] + jnp.dot(low, weight, preferred_element_type=F32)
        total = total + jnp.dot(high, weight, preferred_element_type=F32)
        step[:, lanes] = jnp.maximum(total, 0.0) + jnp.log1p(jnp.exp(-jnp.abs(total)))
        return carry

    lax.fori_loop(0, DI // 256, steps, 0)
    m1 = sub % 4 >= 1
    m2 = sub % 4 >= 2

    def rows_of(t):
        return pl.ds(pl.multiple_of(t * CHUNKS, CHUNKS), CHUNKS)

    def rates_of(lanes):
        return [jnp.broadcast_to(rate2[n : n + 1, lanes], full) for n in range(NS)]

    def block_states(tile, carry):
        lanes = lanes_of(tile)
        rates = rates_of(lanes)

        def one(t, held):
            states, total = held
            rows = rows_of(t)
            now = step[rows, lanes]
            drive = now * signal[rows, lanes]
            states = tuple(
                jnp.exp2(now * rates[n]) * states[n] + in_b[n, rows, :] * drive for n in range(NS)
            )
            return states, total + now

        states, total = lax.fori_loop(0, STEPS, one, ((zero,) * NS, zero), unroll=4)
        sum1 = total + jnp.where(m1, pltpu.roll(total, 1, 0), 0.0)
        sum2 = sum1 + jnp.where(m2, pltpu.roll(sum1, 2, 0), 0.0)
        reach[:, lanes] = jnp.where(m1, pltpu.roll(sum2, 1, 0), 0.0)
        ends = jnp.where(
            sub < 4, jnp.broadcast_to(sum2[3:4], full), jnp.broadcast_to(sum2[7:8], full)
        )
        group = tile // 3
        place = tile % 3
        for h in range(4):
            state_out = zero
            rate_out = zero
            for q in range(4):
                n = 4 * h + q
                decay = jnp.exp2(rates[n] * total)
                one_s = states[n] + jnp.where(m1, decay * pltpu.roll(states[n], 1, 0), 0.0)
                decay2 = jnp.exp2(rates[n] * sum1)
                two_s = one_s + jnp.where(m2, decay2 * pltpu.roll(one_s, 2, 0), 0.0)
                inner[n, :, lanes] = jnp.where(m1, pltpu.roll(two_s, 1, 0), 0.0)
                turn = (q + 5) % 8
                moved = pltpu.roll(two_s, turn, 0) if turn else two_s
                state_out = jnp.where(sub % 4 == q, moved, state_out)
                rate_out = jnp.where(sub % 4 == q, rates[n], rate_out)
            sends[group * 4 + h, place] = state_out
            sends[group * 4 + h, 3] = jnp.where(sub % 4 == place, ends, sends[group * 4 + h, 3])
            rate_own[h, tile] = rate_out
        return carry

    def to_owner(peer):
        return remote(sends.at[peer], recv.at[s], sa.at[peer], ra.at[s], (f, peer))

    def one_group(g, carry):
        lax.fori_loop(g * 3, g * 3 + 3, block_states, 0)
        for h in range(4):
            peer = g * 4 + h

            @pl.when(peer != s)
            def _():
                to_owner(peer).start()

        return carry

    lax.fori_loop(0, 4, one_group, 0)
    recv[s] = sends[s]
    spread_columns(proj, DTR + NS, out_b)

    def own_outputs(tile, carry):
        lanes = lanes_of(tile)
        rates = rates_of(lanes)
        skip = jnp.broadcast_to(wfa[6:7, lanes], full)

        def one(t, held):
            states, total = held
            rows = rows_of(t)
            now = step[rows, lanes]
            sig = signal[rows, lanes]
            drive = now * sig
            total = total + now
            states = tuple(
                jnp.exp2(now * rates[n]) * states[n] + in_b[n, rows, :] * drive for n in range(NS)
            )
            coeffs = [out_b[n, rows, :] for n in range(NS)]
            terms = [coeffs[n] * states[n] for n in range(NS)]
            for n in range(NS):
                grown[n, rows, lanes] = coeffs[n] * jnp.exp2(total * rates[n])
            while len(terms) > 1:
                terms = [a + b for a, b in zip(terms[::2], terms[1::2])]
            y[rows, lanes] = terms[0] + skip * sig
            return states, total

        states = tuple(inner[n, :, lanes] for n in range(NS))
        lax.fori_loop(0, STEPS, one, (states, reach[:, lanes]), unroll=2)
        return carry

    lax.fori_loop(0, 3, own_outputs, 0)
    for d in range(1, width):
        peer = (s + d) % width
        remote(sends.at[peer], recv.at[peer], sa.at[peer], ra.at[peer], (f, peer)).wait_recv()

    def turned(v):
        return pltpu.roll(v, 4, len(v.shape) - 2)

    my_group = s // 4
    my_rates = rate_own[s % 4, pl.ds(my_group * 3, 3)]

    def decays(sums):
        spread = [jnp.broadcast_to(sums[i : i + 1], full) for i in range(3)]
        return jnp.exp2(my_rates * jnp.stack(spread))

    def through(j, carry):
        e, passed = carry
        scan_e[j] = e
        scan_t[j] = passed
        block = order[j]
        got = recv[lax.shift_right_logical(block, 1)]
        odd = jnp.full((4, CHUNKS, LANES), block & 1, jnp.int32) == 1
        got = jnp.where(odd, turned(got), got)
        return decays(got[3]) * e + got[0:3], passed + got[3]

    zero3 = jnp.zeros(slot, F32)
    unit3 = jnp.ones(slot, F32)
    e, passed = lax.fori_loop(0, NBF, through, (zero3, zero), unroll=8)
    p = decays(passed)
    pk1[...] = jnp.where(sub3 < 4, p, turned(e))
    got1[seat] = pk1[...]
    level1 = []
    for d in range(1, SEATS):
        level1.append(push(pk1, got1.at[seat], sb1.at[d], rb1.at[d], (near(d), s)))

    def pack(d, carry):
        i0 = where_to[2 * d]
        i1 = where_to[2 * d + 1]
        bsend[d, 0:3] = jnp.where(sub3 < 4, scan_e[i0], turned(scan_e[i1]))
        bsend[d, 3] = jnp.where(sub < 4, scan_t[i0], turned(scan_t[i1]))
        return carry

    lax.fori_loop(0, width, pack, 0, unroll=4)
    back[s] = bsend[s]
    returns = []
    for d in range(1, width):
        peer = (s + d) % width
        returns.append(push(bsend.at[peer], back.at[s], sd.at[peer], rd.at[s], (f, peer)))
    lax.fori_loop(3, 6, own_outputs, 0)
    for copy in sent[: len(sent) // 2]:
        copy.wait_send()
    for copy in level1:
        copy.wait_recv()

    def gather_near(m, carry):
        e_in, p_in, e_all, p_all = carry
        got = got1[m]
        moved = turned(got)
        early = jnp.full(slot, m, jnp.int32) < jnp.full(slot, seat, jnp.int32)
        e_in = jnp.where(early, got * e_in + moved, e_in)
        p_in = jnp.where(early, got * p_in, p_in)
        return e_in, p_in, got * e_all + moved, got * p_all

    begin = (zero3, unit3, zero3, unit3)
    e_in, p_in, e_all, p_all = lax.fori_loop(0, SEATS, gather_near, begin, unroll=SEATS)
    pk2[...] = jnp.where(sub3 < 4, p_all, turned(e_all))
    got2[part] = pk2[...]
    level2 = []
    for d in range(1, outer):
        level2.append(push(pk2, got2.at[part], sc.at[d], rc.at[d], (far(d), s)))
    lax.fori_loop(6, 9, own_outputs, 0)
    for copy in sent[len(sent) // 2 :] + level1:
        copy.wait_send()
    for copy in level2:
        copy.wait_recv()

    def gather_far(m, start):
        got = got2[m]
        early = jnp.full(slot, m, jnp.int32) < jnp.full(slot, part, jnp.int32)
        return jnp.where(early, got * start + turned(got), start)

    start = lax.fori_loop(0, outer, gather_far, zero3, unroll=4)
    start = p_in * start + e_in

    first = jnp.where(sub < 4, start[0], turned(start[1]))
    fsend[...] = jnp.concatenate([first, start[2]], axis=0).astype(BF16)
    fback[s] = fsend[...]
    starts = []
    for d in range(1, width):
        peer = (s + d) % width
        starts.append(push(fsend, fback.at[s], sf.at[peer], rf.at[s], (f, peer)))
    lax.fori_loop(9, 12, own_outputs, 0)
    for copy in level2 + returns:
        copy.wait_send()
    for d in range(1, width):
        to_owner((s + d) % width).wait_send()
    for d in range(1, width):
        peer = (s + d) % width
        remote(bsend.at[peer], back.at[peer], sd.at[peer], rd.at[peer], (f, peer)).wait_recv()

    def both(tile8, r):
        return jnp.where(
            sub < 4,
            jnp.broadcast_to(tile8[r : r + 1], full),
            jnp.broadcast_to(tile8[4 + r : 5 + r], full),
        )

    def complete(g, place):
        lanes = lanes_of(g * 3 + place)
        rates = rates_of(lanes)
        passed = both(back[g * 4, 3], place)
        entering = []
        for h in range(4):
            came = back[g * 4 + h, place]
            begun = fback[g * 4 + h].astype(F32)
            for q in range(4):
                r = place * 4 + q
                line = jnp.broadcast_to(begun[r : r + 1], full)
                entering.append(both(came, q) + jnp.exp2(rates[4 * h + q] * passed) * line)

        def one(t, carry):
            rows = rows_of(t)
            terms = [grown[n, rows, lanes] * entering[n] for n in range(NS)]
            while len(terms) > 1:
                terms = [a + b for a, b in zip(terms[::2], terms[1::2])]
            scanned = (y[rows, lanes] + terms[0]).astype(BF16).astype(F32)
            y[rows, lanes] = scanned * gz[rows, lanes]
            return carry

        lax.fori_loop(0, STEPS, one, 0, unroll=4)
        gated[:, lanes] = y[:, lanes].astype(BF16)

    undo = token_rows()

    def one_group_back(g, carry):
        for h in range(4):
            peer = g * 4 + h

            @pl.when(peer != s)
            def _():
                remote(fsend, fback.at[peer], sf.at[peer], rf.at[peer], (f, peer)).wait_recv()

        for place in range(3):
            complete(g, place)
        lanes = lanes_of(g, 3 * LANES)
        out[:, lanes] = jnp.dot(undo, gated[:, lanes], preferred_element_type=F32).astype(BF16)
        return carry

    lax.fori_loop(0, 4, one_group_back, 0)
    for copy in starts:
        copy.wait_send()


def shards(
    inner_x,
    inner_z,
    conv_weight,
    conv_bias,
    proj_weight,
    step_weight,
    step_bias,
    decay_log,
    skip_gain,
    out_weight,
    order_table,
):
    frames, rows, columns, channels = inner_x.shape
    space = lax.axis_size("space")
    outer = lax.axis_size("tm") // SEATS
    dma = pltpu.SemaphoreType.DMA
    slot = (3, CHUNKS, LANES)
    anyw = pl.BlockSpec(memory_space=pl.ANY)
    vm = pl.BlockSpec(memory_space=pltpu.VMEM)
    held = [
        ((TOK, DI), BF16),
        ((TOK, DI), BF16),
        ((space, WROWS, CH), F32),
        ((space, CH, LANES), BF16),
        ((space, PAIR, LANES), BF16),
        ((PAIR, LANES), F32),
        ((CH, LANES), F32),
        ((TROWS, LANES), F32),
        ((TROWS, LANES), BF16),
        ((TROWS, LANES), BF16),
        None,
        ((WROWS, DI), F32),
        ((WB, DI), F32),
        ((2, BLK + 8, DI), F32),
        ((TOK, DI), BF16),
        ((TOK, DI), F32),
        ((TOK, DI), F32),
        ((TOK, DI), F32),
        ((NS, DI), F32),
        ((4, TILES, CHUNKS, LANES), F32),
        ((NS, TOK, LANES), F32),
        ((NS, TOK, LANES), F32),
        ((NS, CHUNKS, DI), F32),
        ((CHUNKS, DI), F32),
        ((TOK, DI), F32),
        ((TOK, DI), BF16),
        ((NS, TOK, DI), F32),
        ((space, 4, CHUNKS, LANES), F32),
        ((space, 4, CHUNKS, LANES), F32),
        ((NBF,) + slot, F32),
        ((NBF, CHUNKS, LANES), F32),
        (slot, F32),
        ((SEATS,) + slot, F32),
        (slot, F32),
        ((outer,) + slot, F32),
        ((space, 4, CHUNKS, LANES), F32),
        ((space, 4, CHUNKS, LANES), F32),
        ((16, LANES), BF16),
        ((space, 16, LANES), BF16),
    ]
    scratch = [pltpu.SMEM((NBF,), jnp.int32) if h is None else pltpu.VMEM(*h) for h in held]
    scratch += [dma((2,))] + [dma((3, 8))] * 4 + [dma] * 2
    scratch += [dma((16,))] * 2 + [dma((8,))] * 4 + [dma((16,))] * 4
    gated = pl.pallas_call(
        layer,
        out_shape=jax.ShapeDtypeStruct((TOK, DI), BF16),
        in_specs=[anyw, anyw] + [vm] * 7 + [pl.BlockSpec(memory_space=pltpu.SMEM)],
        out_specs=vm,
        scratch_shapes=scratch,
        compiler_params=pltpu.CompilerParams(
            collective_id=0, has_side_effects=True, vmem_limit_bytes=VMEM_LIMIT
        ),
        name="layer",
    )(
        inner_x.reshape(TOK, DI),
        inner_z.reshape(TOK, DI),
        conv_weight,
        conv_bias.reshape(1, CH),
        proj_weight.T,
        step_weight,
        step_bias.reshape(1, CH),
        decay_log,
        skip_gain.reshape(1, CH),
        order_table,
    )
    mixed = jnp.dot(gated, out_weight, preferred_element_type=F32).astype(BF16)
    return mixed.reshape(frames, rows, columns, D)


def solution(mesh):
    in_specs = (
        P("tm", "space", None, None),
        P("tm", "space", None, None),
        P(None, "space"),
        P("space"),
        P("space", None),
        P(None, "space"),
        P("space"),
        P(None, "space"),
        P("space"),
        P(),
        P(),
    )
    out_specs = P("tm", "space", None, None)
    return jax.shard_map(shards, mesh=mesh, in_specs=in_specs, out_specs=out_specs, check_vma=False)
```

```python
import jax
import jax.numpy as jnp
from jax import lax
from jax.experimental import pallas as pl
from jax.experimental.pallas import tpu as pltpu
from jax.sharding import PartitionSpec as P

MESH = pl.DeviceIdType.MESH
NS = 16
DTR = 48
KC = 4
BLK = 128
NBF = 32
DI = 1536
D = 768
TOK = 256
CH = 96
LANES = 128
TILES = DI // LANES
CHUNKS = 8
STEPS = TOK // CHUNKS
WROWS = 24
TROWS = 48
TAIL = (KC - 1) * TILES
PAIR = 80
WB = DTR + DTR + 2 * NS
SEATS = 8
VMEM_LIMIT = 56 * 1024 * 1024
LOG2E = 1.4426950408889634
F32 = jnp.float32
BF16 = jnp.bfloat16


def scan_rows():
    r = lax.broadcasted_iota(jnp.int32, (TOK, TOK), 0)
    i = lax.broadcasted_iota(jnp.int32, (TOK, TOK), 1)
    return ((r & (CHUNKS - 1)) * STEPS + (r >> 3) == i).astype(F32).astype(BF16)


def token_rows():
    i = lax.broadcasted_iota(jnp.int32, (TOK, TOK), 0)
    r = lax.broadcasted_iota(jnp.int32, (TOK, TOK), 1)
    return ((r & (CHUNKS - 1)) * STEPS + (r >> 3) == i).astype(F32).astype(BF16)


def silu(v):
    half = 0.5 * v
    return half + half * jnp.tanh(half)


def lanes_of(tile, width=LANES):
    return pl.ds(pl.multiple_of(tile * width, width), width)


def spread_columns(projected, first, out):
    for n in range(NS):
        out[n] = jnp.broadcast_to(projected[:, first + n : first + n + 1], (TOK, LANES))


def layer(
    x, z, cw, cb, pwt, sw, sb, dl, sg, order, out,
    xv, zv, gwf, gwb, gt, tstage, wstage, tsel, tsend, trecv, where_to,
    wfa, wba, xf, sigt, gz, signal, step, rate2, rate_own, in_b, out_b, inner, reach, y, gated, grown,
    sends, recv, scan_e, scan_t, pk1, got1, pk2, got2, bsend, back, fsend, fback,
    local, s1, r1, s2, r2, st, rt, sa, ra, sb1, rb1, sc, rc, sd, rd, sf, rf, up, down,
):
    f = lax.axis_index("tm")
    s = lax.axis_index("space")
    frames = lax.axis_size("tm")
    width = lax.axis_size("space")
    outer = frames // SEATS
    row = s // 4
    side = s // 2 % 2
    core = s % 2
    part = f // SEATS
    seat = f % SEATS
    sibling = (f, s - core + 1 - core)
    twin = f + 1 - f % 2 * 2
    ahead = ((f + 1) % frames, s)
    behind = ((f + frames - 1) % frames, s)
    full = (CHUNKS, LANES)
    slot = (3, CHUNKS, LANES)
    sub = lax.broadcasted_iota(jnp.int32, full, 0)
    sub3 = lax.broadcasted_iota(jnp.int32, slot, 1)
    zero = jnp.zeros(full, F32)

    def chip(dx, dy):
        return (row + dx) % 4 * 4 + (side + dy) % 2 * 2 + core

    def near(d):
        return part * SEATS + (seat + d) % SEATS

    def far(d):
        return ((part + d) % outer) * SEATS + seat

    def remote(src, dst, ssem, rsem, target):
        return pltpu.make_async_remote_copy(
            src_ref=src,
            dst_ref=dst,
            send_sem=ssem,
            recv_sem=rsem,
            device_id=target,
            device_id_type=MESH,
        )

    def push(src, dst, ssem, rsem, target):
        copy = remote(src, dst, ssem, rsem, target)
        copy.start()
        return copy

    load_x = pltpu.make_async_copy(x, xv, local.at[0])
    load_z = pltpu.make_async_copy(z, zv, local.at[1])
    load_x.start()

    barrier = pltpu.get_barrier_semaphore()
    for d in range(1, width):
        pl.semaphore_signal(barrier, inc=1, device_id=(f, (s + d) % width), device_id_type=MESH)
    for d in range(1, SEATS):
        pl.semaphore_signal(barrier, inc=1, device_id=(near(d), s), device_id_type=MESH)
    above = ((f + 2) % frames, s)
    below = ((f + frames - 2) % frames, s)
    for neighbour in (above, below):
        pl.semaphore_signal(barrier, inc=1, device_id=neighbour, device_id_type=MESH)
    pl.semaphore_signal(barrier, inc=1, device_id=behind, device_id_type=MESH)
    for dx in range(4):
        pl.semaphore_signal(barrier, inc=1, device_id=(twin, chip(dx, 1)), device_id_type=MESH)

    load_z.start()
    gwf[s, 0:KC] = cw[...]
    gwf[s, KC : KC + 1] = cb[...]
    gwf[s, 5:6] = sb[...]
    gwf[s, 6:7] = sg[...]
    gwf[s, 7:8] = jnp.zeros((1, CH), F32)
    gwf[s, 8:WROWS] = dl[...]
    narrow = pwt[...].astype(F32)
    wstage[0:DTR, 0:CH] = sw[...].astype(F32)
    wstage[DTR:CH, 0:CH] = narrow[0:DTR]
    for m in range(3):
        wstage[32 * m : 32 * (m + 1), CH:LANES] = narrow[DTR:, 32 * m : 32 * (m + 1)]
    gwb[s] = wstage[...].astype(BF16)
    tstage[...] = jnp.zeros_like(tstage)
    pl.semaphore_wait(barrier, width + SEATS + 5)

    def place(a, i):
        return (gwf.at[i], gt.at[i], gwb.at[i])[a]

    sent = []
    relayed = [0, 0, 0]

    def relay(a, dx, dy, tx, ty):
        ref = place(a, chip(dx, dy))
        landing = (dx - tx) % 4 * 2 + (dy - ty) % 2
        ssem = s1.at[a, relayed[a]]
        relayed[a] += 1
        frame = twin if ty and a != 1 else f
        sent.append(push(ref, ref, ssem, r1.at[a, landing], (frame, chip(tx, ty))))

    def tail_of(block):
        pair = gt[lax.shift_right_logical(block, 1)].astype(F32)
        odd = jnp.full((TAIL, LANES), block & 1, jnp.int32) == 1
        return jnp.where(odd, pair[TAIL : 2 * TAIL], pair[0:TAIL])

    def share(a, dx, dy):
        ref = place(a, chip(dx, dy))
        k = dx * 2 + dy
        sent.append(push(ref, ref, s2.at[a, k], r2.at[a, k], sibling))

    def take(a, dx, dy):
        ref = place(a, chip(dx, dy))
        remote(ref, ref, s1.at[a, 0], r1.at[a, dx * 2 + dy], sibling).wait_recv()

    def offer(a, targets):
        for tx, ty in targets:
            relay(a, 0, 0, tx, ty)
        share(a, 0, 0)

    def collect(a, items):
        for dx, dy in items:
            take(a, dx, dy)
            share(a, dx, dy)

    def other_side(a):
        take(a, 0, 1)
        relay(a, 0, 1, 1, 0)
        relay(a, 0, 1, 3, 0)
        if a == 1:
            relay(a, 0, 1, 2, 0)
        share(a, 0, 1)

    def neighbours(a):
        for dy in range(2):
            take(a, 1, dy)
            relay(a, 1, dy, 3, 0)
            share(a, 1, dy)
        for dy in range(2):
            take(a, 3, dy)
            share(a, 3, dy)

    def opposite(a):
        for dy in range(2):
            take(a, 2, dy)
            share(a, 2, dy)

    def from_sibling(a):
        for dx in range(4):
            for dy in range(2):
                ref = place(a, chip(dx, dy) - core + 1 - core)
                k = dx * 2 + dy
                remote(ref, ref, s2.at[a, k], r2.at[a, k], sibling).wait_recv()

    offer(0, ((0, 1), (1, 1), (3, 1), (2, 1), (1, 0), (3, 0), (2, 0)))
    load_x.wait()
    for b in range(2):
        ends = xv[BLK * (b + 1) - 16 : BLK * (b + 1)].astype(F32)
        for t in range(KC - 1):
            for j in range(TILES):
                line = ends[13 + t : 14 + t, LANES * j : LANES * (j + 1)]
                at = b * TAIL + t * TILES + j
                tstage[at : at + 1] = line
    gt[s] = tstage[...].astype(BF16)
    offer(1, ((0, 1), (2, 0), (1, 0), (3, 0)))
    offer(2, ((0, 1), (1, 0), (3, 0)))
    passed_on = [0]

    def pass_ready():
        k = passed_on[0]
        if 0 < k <= 7:
            pl.semaphore_wait(up, 1)
        if 0 < k <= 3:
            pl.semaphore_wait(down, 1)
        if k < 7:
            pl.semaphore_signal(up, inc=1, device_id=below, device_id_type=MESH)
        if k < 3:
            pl.semaphore_signal(down, inc=1, device_id=above, device_id_type=MESH)
        passed_on[0] += 1

    pass_ready()
    listed = [order[j] for j in range(NBF)]

    def inverse(r, carry):
        found = 0
        for j in range(NBF):
            found = jnp.where(listed[j] == r, j, found)
        where_to[r] = found
        return carry

    lax.fori_loop(0, NBF, inverse, 0)
    for b in range(2):
        xf[b, 0:8] = jnp.zeros((8, DI), F32)

    def widen(tile, carry):
        lanes = lanes_of(tile)
        for b in range(2):
            xf[b, 8 : 8 + BLK, lanes] = xv[BLK * b : BLK * (b + 1), lanes].astype(F32)
        return carry

    lax.fori_loop(0, TILES, widen, 0)
    sends[...] = jnp.zeros_like(sends)
    other_side(1)
    other_side(2)
    pass_ready()
    collect(0, ((3, 0), (1, 0), (0, 1), (3, 1), (1, 1), (2, 0), (2, 1)))
    collect(1, ((1, 0), (3, 0), (2, 0), (1, 1), (3, 1), (2, 1)))
    pass_ready()
    from_sibling(0)
    for i in range(DI // CH):
        wfa[:, CH * i : CH * (i + 1)] = gwf[i]

    def filtered(b, count, lanes):
        total = wfa[4:5, lanes]
        for k in range(KC):
            total = total + wfa[k : k + 1, lanes] * xf[b, 5 + k : 5 + k + count, lanes]
        return silu(total).astype(BF16)

    def convolve(tile, carry):
        lanes = lanes_of(tile)
        for b in range(2):
            sigt[BLK * b : BLK * (b + 1), lanes] = filtered(b, BLK, lanes)
        return carry

    lax.fori_loop(0, 3, convolve, 0)
    pass_ready()
    neighbours(2)
    lax.fori_loop(3, 6, convolve, 0)
    from_sibling(1)
    tsel[...] = jnp.zeros_like(tsel)
    tsel[0:TAIL] = tail_of(order[NBF - 1])
    tsend[...] = tsel[...].astype(BF16)
    sent_tail = push(tsend, trecv, st, rt, ahead)
    sent.append(sent_tail)
    opposite(2)
    lax.fori_loop(6, TILES, convolve, 0)
    pass_ready()
    rate2[...] = -jnp.exp(wfa[8:WROWS]) * LOG2E
    rearranged = scan_rows()
    load_z.wait()

    def gate(chunk, carry):
        lanes = lanes_of(chunk, 256)
        zs = jnp.dot(rearranged, zv[:, lanes], preferred_element_type=F32)
        gz[:, lanes] = silu(zs)
        return carry

    lax.fori_loop(0, DI // 256, gate, 0)
    pass_ready()
    from_sibling(2)
    for i in range(DI // CH):
        held = gwb[i].astype(F32)
        wba[0:CH, CH * i : CH * (i + 1)] = held[:, 0:CH]
        for m in range(3):
            at = CH * i + 32 * m
            wba[CH:WB, at : at + 32] = held[32 * m : 32 * (m + 1), CH:LANES]
    sent_tail.wait_recv()
    came = trecv[...].astype(F32)[0:TAIL]
    came = jnp.where(jnp.full(came.shape, f, jnp.int32) == 0, 0.0, came)
    for b in range(2):
        at = where_to[2 * s + b]
        found = tail_of(order[jnp.maximum(at - 1, 0)])
        halo = jnp.where(jnp.full(came.shape, at, jnp.int32) == 0, came, found)
        for t in range(KC - 1):
            for j in range(TILES):
                line = halo[t * TILES + j : t * TILES + j + 1]
                xf[b, 5 + t : 6 + t, LANES * j : LANES * (j + 1)] = line

    def heads(tile, carry):
        lanes = lanes_of(tile)
        for b in range(2):
            sigt[BLK * b : BLK * b + 16, lanes] = filtered(b, 16, lanes)
        return carry

    lax.fori_loop(0, TILES, heads, 0)

    def rearrange(chunk, carry):
        lanes = lanes_of(chunk, 256)
        signal[:, lanes] = jnp.dot(rearranged, sigt[:, lanes], preferred_element_type=F32)
        return carry

    lax.fori_loop(0, DI // 256, rearrange, 0)
    pass_ready()
    proj = lax.dot_general(
        signal[...].astype(BF16),
        wba[DTR:WB].astype(BF16),
        (((1,), (1,)), ((), ())),
        preferred_element_type=F32,
    )
    spread_columns(proj, DTR, in_b)
    rank = proj[:, :DTR]
    high = rank.astype(BF16)
    low = (rank - high.astype(F32)).astype(BF16)

    def steps(chunk, carry):
        lanes = lanes_of(chunk, 256)
        weight = wba[0:DTR, lanes].astype(BF16)
        total = wfa[5:6, lanes] + jnp.dot(low, weight, preferred_element_type=F32)
        total = total + jnp.dot(high, weight, preferred_element_type=F32)
        step[:, lanes] = jnp.maximum(total, 0.0) + jnp.log1p(jnp.exp(-jnp.abs(total)))
        return carry

    lax.fori_loop(0, DI // 256, steps, 0)
    pass_ready()
    m1 = sub % 4 >= 1
    m2 = sub % 4 >= 2

    def rows_of(t):
        return pl.ds(pl.multiple_of(t * CHUNKS, CHUNKS), CHUNKS)

    def rates_of(lanes):
        return [jnp.broadcast_to(rate2[n : n + 1, lanes], full) for n in range(NS)]

    def block_states(tile, carry):
        lanes = lanes_of(tile)
        rates = rates_of(lanes)

        def one(t, held):
            states, total = held
            rows = rows_of(t)
            now = step[rows, lanes]
            drive = now * signal[rows, lanes]
            states = tuple(
                jnp.exp2(now * rates[n]) * states[n] + in_b[n, rows, :] * drive for n in range(NS)
            )
            return states, total + now

        states, total = lax.fori_loop(0, STEPS, one, ((zero,) * NS, zero), unroll=4)
        sum1 = total + jnp.where(m1, pltpu.roll(total, 1, 0), 0.0)
        sum2 = sum1 + jnp.where(m2, pltpu.roll(sum1, 2, 0), 0.0)
        reach[:, lanes] = jnp.where(m1, pltpu.roll(sum2, 1, 0), 0.0)
        ends = jnp.where(
            sub < 4, jnp.broadcast_to(sum2[3:4], full), jnp.broadcast_to(sum2[7:8], full)
        )
        group = tile // 3
        place = tile % 3
        for h in range(4):
            state_out = zero
            rate_out = zero
            for q in range(4):
                n = 4 * h + q
                decay = jnp.exp2(rates[n] * total)
                one_s = states[n] + jnp.where(m1, decay * pltpu.roll(states[n], 1, 0), 0.0)
                decay2 = jnp.exp2(rates[n] * sum1)
                two_s = one_s + jnp.where(m2, decay2 * pltpu.roll(one_s, 2, 0), 0.0)
                inner[n, :, lanes] = jnp.where(m1, pltpu.roll(two_s, 1, 0), 0.0)
                turn = (q + 5) % 8
                moved = pltpu.roll(two_s, turn, 0) if turn else two_s
                state_out = jnp.where(sub % 4 == q, moved, state_out)
                rate_out = jnp.where(sub % 4 == q, rates[n], rate_out)
            owner = h * 4 + group
            sends[owner, place] = state_out
            sends[owner, 3] = jnp.where(sub % 4 == place, ends, sends[owner, 3])
            rate_own[h, tile] = rate_out
        return carry

    def to_owner(peer):
        return remote(sends.at[peer], recv.at[s], sa.at[peer], ra.at[s], (f, peer))

    def one_group(g, carry):
        lax.fori_loop(g * 3, g * 3 + 3, block_states, 0)
        for h in range(4):
            peer = h * 4 + g

            @pl.when(peer != s)
            def _():
                to_owner(peer).start()

        return carry

    lax.fori_loop(0, 4, one_group, 0)
    recv[s] = sends[s]
    spread_columns(proj, DTR + NS, out_b)

    def own_outputs(tile, carry):
        lanes = lanes_of(tile)
        rates = rates_of(lanes)
        skip = jnp.broadcast_to(wfa[6:7, lanes], full)

        def one(t, held):
            states, total = held
            rows = rows_of(t)
            now = step[rows, lanes]
            sig = signal[rows, lanes]
            drive = now * sig
            total = total + now
            states = tuple(
                jnp.exp2(now * rates[n]) * states[n] + in_b[n, rows, :] * drive for n in range(NS)
            )
            coeffs = [out_b[n, rows, :] for n in range(NS)]
            terms = [coeffs[n] * states[n] for n in range(NS)]
            for n in range(NS):
                grown[n, rows, lanes] = coeffs[n] * jnp.exp2(total * rates[n])
            while len(terms) > 1:
                terms = [a + b for a, b in zip(terms[::2], terms[1::2])]
            y[rows, lanes] = terms[0] + skip * sig
            return states, total

        states = tuple(inner[n, :, lanes] for n in range(NS))
        lax.fori_loop(0, STEPS, one, (states, reach[:, lanes]), unroll=2)
        return carry

    lax.fori_loop(0, 3, own_outputs, 0)
    for d in range(1, width):
        peer = (s + d) % width
        remote(sends.at[peer], recv.at[peer], sa.at[peer], ra.at[peer], (f, peer)).wait_recv()

    def turned(v):
        return pltpu.roll(v, 4, len(v.shape) - 2)

    my_group = s % 4
    my_rates = rate_own[s // 4, pl.ds(my_group * 3, 3)]

    def decays(sums):
        spread = [jnp.broadcast_to(sums[i : i + 1], full) for i in range(3)]
        return jnp.exp2(my_rates * jnp.stack(spread))

    def through(j, carry):
        e, passed = carry
        scan_e[j] = e
        scan_t[j] = passed
        block = order[j]
        got = recv[lax.shift_right_logical(block, 1)]
        odd = jnp.full((4, CHUNKS, LANES), block & 1, jnp.int32) == 1
        got = jnp.where(odd, turned(got), got)
        return decays(got[3]) * e + got[0:3], passed + got[3]

    zero3 = jnp.zeros(slot, F32)
    unit3 = jnp.ones(slot, F32)
    e, passed = lax.fori_loop(0, NBF, through, (zero3, zero), unroll=8)
    p = decays(passed)
    pk1[...] = jnp.where(sub3 < 4, p, turned(e))
    got1[seat] = pk1[...]
    level1 = []
    for d in range(1, SEATS):
        level1.append(push(pk1, got1.at[seat], sb1.at[d], rb1.at[d], (near(d), s)))

    def pack(d, carry):
        i0 = where_to[2 * d]
        i1 = where_to[2 * d + 1]
        bsend[d, 0:3] = jnp.where(sub3 < 4, scan_e[i0], turned(scan_e[i1]))
        bsend[d, 3] = jnp.where(sub < 4, scan_t[i0], turned(scan_t[i1]))
        return carry

    lax.fori_loop(0, width, pack, 0, unroll=4)
    lax.fori_loop(3, 6, own_outputs, 0)
    for copy in sent[: len(sent) // 2]:
        copy.wait_send()
    for copy in level1:
        copy.wait_recv()

    def gather_near(m, carry):
        e_in, p_in, e_all, p_all = carry
        got = got1[m]
        moved = turned(got)
        early = jnp.full(slot, m, jnp.int32) < jnp.full(slot, seat, jnp.int32)
        e_in = jnp.where(early, got * e_in + moved, e_in)
        p_in = jnp.where(early, got * p_in, p_in)
        return e_in, p_in, got * e_all + moved, got * p_all

    begin = (zero3, unit3, zero3, unit3)
    e_in, p_in, e_all, p_all = lax.fori_loop(0, SEATS, gather_near, begin, unroll=SEATS)
    pk2[...] = jnp.where(sub3 < 4, p_all, turned(e_all))
    got2[part] = pk2[...]
    level2 = []
    for d in range(1, outer):
        level2.append(push(pk2, got2.at[part], sc.at[d], rc.at[d], (far(d), s)))
    back[s] = bsend[s]
    returns = []
    for d in range(1, width):
        peer = (s + d) % width
        returns.append(push(bsend.at[peer], back.at[s], sd.at[peer], rd.at[s], (f, peer)))
    lax.fori_loop(6, 9, own_outputs, 0)
    for copy in sent[len(sent) // 2 :] + level1:
        copy.wait_send()
    for copy in level2:
        copy.wait_recv()

    def gather_far(m, start):
        got = got2[m]
        early = jnp.full(slot, m, jnp.int32) < jnp.full(slot, part, jnp.int32)
        return jnp.where(early, got * start + turned(got), start)

    start = lax.fori_loop(0, outer, gather_far, zero3, unroll=4)
    start = p_in * start + e_in

    first = jnp.where(sub < 4, start[0], turned(start[1]))
    fsend[...] = jnp.concatenate([first, start[2]], axis=0).astype(BF16)
    fback[s] = fsend[...]
    starts = []
    for d in range(1, width):
        peer = (s + d) % width
        starts.append(push(fsend, fback.at[s], sf.at[peer], rf.at[s], (f, peer)))
    lax.fori_loop(9, 12, own_outputs, 0)
    for copy in level2 + returns:
        copy.wait_send()
    for d in range(1, width):
        to_owner((s + d) % width).wait_send()
    for d in range(1, width):
        peer = (s + d) % width
        remote(bsend.at[peer], back.at[peer], sd.at[peer], rd.at[peer], (f, peer)).wait_recv()

    def both(tile8, r):
        return jnp.where(
            sub < 4,
            jnp.broadcast_to(tile8[r : r + 1], full),
            jnp.broadcast_to(tile8[4 + r : 5 + r], full),
        )

    def complete(g, place):
        lanes = lanes_of(g * 3 + place)
        rates = rates_of(lanes)
        passed = both(back[g, 3], place)
        entering = []
        for h in range(4):
            came = back[h * 4 + g, place]
            begun = fback[h * 4 + g].astype(F32)
            for q in range(4):
                r = place * 4 + q
                line = jnp.broadcast_to(begun[r : r + 1], full)
                entering.append(both(came, q) + jnp.exp2(rates[4 * h + q] * passed) * line)

        def one(t, carry):
            rows = rows_of(t)
            terms = [grown[n, rows, lanes] * entering[n] for n in range(NS)]
            while len(terms) > 1:
                terms = [a + b for a, b in zip(terms[::2], terms[1::2])]
            scanned = (y[rows, lanes] + terms[0]).astype(BF16).astype(F32)
            y[rows, lanes] = scanned * gz[rows, lanes]
            return carry

        lax.fori_loop(0, STEPS, one, 0, unroll=4)
        gated[:, lanes] = y[:, lanes].astype(BF16)

    undo = token_rows()

    def one_group_back(g, carry):
        for h in range(4):
            peer = h * 4 + g

            @pl.when(peer != s)
            def _():
                remote(fsend, fback.at[peer], sf.at[peer], rf.at[peer], (f, peer)).wait_recv()

        for place in range(3):
            complete(g, place)
        lanes = lanes_of(g, 3 * LANES)
        out[:, lanes] = jnp.dot(undo, gated[:, lanes], preferred_element_type=F32).astype(BF16)
        return carry

    lax.fori_loop(0, 4, one_group_back, 0)
    for copy in starts:
        copy.wait_send()


def shards(
    inner_x,
    inner_z,
    conv_weight,
    conv_bias,
    proj_weight,
    step_weight,
    step_bias,
    decay_log,
    skip_gain,
    out_weight,
    order_table,
):
    frames, rows, columns, channels = inner_x.shape
    space = lax.axis_size("space")
    outer = lax.axis_size("tm") // SEATS
    dma = pltpu.SemaphoreType.DMA
    slot = (3, CHUNKS, LANES)
    anyw = pl.BlockSpec(memory_space=pl.ANY)
    vm = pl.BlockSpec(memory_space=pltpu.VMEM)
    held = [
        ((TOK, DI), BF16),
        ((TOK, DI), BF16),
        ((space, WROWS, CH), F32),
        ((space, CH, LANES), BF16),
        ((space, PAIR, LANES), BF16),
        ((PAIR, LANES), F32),
        ((CH, LANES), F32),
        ((TROWS, LANES), F32),
        ((TROWS, LANES), BF16),
        ((TROWS, LANES), BF16),
        None,
        ((WROWS, DI), F32),
        ((WB, DI), F32),
        ((2, BLK + 8, DI), F32),
        ((TOK, DI), BF16),
        ((TOK, DI), F32),
        ((TOK, DI), F32),
        ((TOK, DI), F32),
        ((NS, DI), F32),
        ((4, TILES, CHUNKS, LANES), F32),
        ((NS, TOK, LANES), F32),
        ((NS, TOK, LANES), F32),
        ((NS, CHUNKS, DI), F32),
        ((CHUNKS, DI), F32),
        ((TOK, DI), F32),
        ((TOK, DI), BF16),
        ((NS, TOK, DI), F32),
        ((space, 4, CHUNKS, LANES), F32),
        ((space, 4, CHUNKS, LANES), F32),
        ((NBF,) + slot, F32),
        ((NBF, CHUNKS, LANES), F32),
        (slot, F32),
        ((SEATS,) + slot, F32),
        (slot, F32),
        ((outer,) + slot, F32),
        ((space, 4, CHUNKS, LANES), F32),
        ((space, 4, CHUNKS, LANES), F32),
        ((16, LANES), BF16),
        ((space, 16, LANES), BF16),
    ]
    scratch = [pltpu.SMEM((NBF,), jnp.int32) if h is None else pltpu.VMEM(*h) for h in held]
    scratch += [dma((2,))] + [dma((3, 8))] * 4 + [dma] * 2
    scratch += [dma((16,))] * 2 + [dma((8,))] * 4 + [dma((16,))] * 4
    scratch += [pltpu.SemaphoreType.REGULAR] * 2
    gated = pl.pallas_call(
        layer,
        out_shape=jax.ShapeDtypeStruct((TOK, DI), BF16),
        in_specs=[anyw, anyw] + [vm] * 7 + [pl.BlockSpec(memory_space=pltpu.SMEM)],
        out_specs=vm,
        scratch_shapes=scratch,
        compiler_params=pltpu.CompilerParams(
            collective_id=0, has_side_effects=True, vmem_limit_bytes=VMEM_LIMIT
        ),
        name="layer",
    )(
        inner_x.reshape(TOK, DI),
        inner_z.reshape(TOK, DI),
        conv_weight,
        conv_bias.reshape(1, CH),
        proj_weight.T,
        step_weight,
        step_bias.reshape(1, CH),
        decay_log,
        skip_gain.reshape(1, CH),
        order_table,
    )
    mixed = jnp.dot(gated, out_weight, preferred_element_type=F32).astype(BF16)
    return mixed.reshape(frames, rows, columns, D)


def solution(mesh):
    in_specs = (
        P("tm", "space", None, None),
        P("tm", "space", None, None),
        P(None, "space"),
        P("space"),
        P("space", None),
        P(None, "space"),
        P("space"),
        P(None, "space"),
        P("space"),
        P(),
        P(),
    )
    out_specs = P("tm", "space", None, None)
    return jax.shard_map(shards, mesh=mesh, in_specs=in_specs, out_specs=out_specs, check_vma=False)
```

```python
import jax
import jax.numpy as jnp
from jax import lax
from jax.experimental import pallas as pl
from jax.experimental.pallas import tpu as pltpu
from jax.sharding import PartitionSpec as P

MESH = pl.DeviceIdType.MESH
NS = 16
DTR = 48
KC = 4
BLK = 128
NBF = 32
DI = 1536
D = 768
TOK = 256
CH = 96
LANES = 128
TILES = DI // LANES
CHUNKS = 8
STEPS = TOK // CHUNKS
WROWS = 24
TROWS = 48
TAIL = (KC - 1) * TILES
PAIR = 80
WB = DTR + DTR + 2 * NS
SEATS = 8
VMEM_LIMIT = 56 * 1024 * 1024
LOG2E = 1.4426950408889634
F32 = jnp.float32
BF16 = jnp.bfloat16


def scan_rows():
    r = lax.broadcasted_iota(jnp.int32, (TOK, TOK), 0)
    i = lax.broadcasted_iota(jnp.int32, (TOK, TOK), 1)
    return ((r & (CHUNKS - 1)) * STEPS + (r >> 3) == i).astype(F32).astype(BF16)


def token_rows():
    i = lax.broadcasted_iota(jnp.int32, (TOK, TOK), 0)
    r = lax.broadcasted_iota(jnp.int32, (TOK, TOK), 1)
    return ((r & (CHUNKS - 1)) * STEPS + (r >> 3) == i).astype(F32).astype(BF16)


def silu(v):
    half = 0.5 * v
    return half + half * jnp.tanh(half)


def lanes_of(tile, width=LANES):
    return pl.ds(pl.multiple_of(tile * width, width), width)


def spread_columns(projected, first, out):
    for n in range(NS):
        out[n] = jnp.broadcast_to(projected[:, first + n : first + n + 1], (TOK, LANES))


def layer(
    x, z, cw, cb, pwt, sw, sb, dl, sg, order, out,
    xv, zv, gwf, gwb, gt, tstage, wstage, tsel, tsend, trecv, where_to,
    wfa, wba, xf, sigt, gz, signal, step, rate2, rate_own, in_b, out_b, inner, reach, y, gated, grown,
    sends, recv, scan_e, scan_t, pk1, got1, pk2, got2, bsend, back, fsend, fback,
    local, s1, r1, s2, r2, st, rt, sa, ra, sb1, rb1, sc, rc, sd, rd, sf, rf,
):
    f = lax.axis_index("tm")
    s = lax.axis_index("space")
    frames = lax.axis_size("tm")
    width = lax.axis_size("space")
    outer = frames // SEATS
    row = s // 4
    side = s // 2 % 2
    core = s % 2
    part = f // SEATS
    seat = f % SEATS
    sibling = (f, s - core + 1 - core)
    twin = f + 1 - f % 2 * 2
    ahead = ((f + 1) % frames, s)
    behind = ((f + frames - 1) % frames, s)
    full = (CHUNKS, LANES)
    slot = (3, CHUNKS, LANES)
    sub = lax.broadcasted_iota(jnp.int32, full, 0)
    sub3 = lax.broadcasted_iota(jnp.int32, slot, 1)
    zero = jnp.zeros(full, F32)

    def chip(dx, dy):
        return (row + dx) % 4 * 4 + (side + dy) % 2 * 2 + core

    def near(d):
        return part * SEATS + (seat + d) % SEATS

    def far(d):
        return ((part + d) % outer) * SEATS + seat

    def remote(src, dst, ssem, rsem, target):
        return pltpu.make_async_remote_copy(
            src_ref=src,
            dst_ref=dst,
            send_sem=ssem,
            recv_sem=rsem,
            device_id=target,
            device_id_type=MESH,
        )

    def push(src, dst, ssem, rsem, target):
        copy = remote(src, dst, ssem, rsem, target)
        copy.start()
        return copy

    load_x = pltpu.make_async_copy(x, xv, local.at[0])
    load_z = pltpu.make_async_copy(z, zv, local.at[1])
    load_x.start()

    barrier = pltpu.get_barrier_semaphore()
    for d in range(1, width):
        pl.semaphore_signal(barrier, inc=1, device_id=(f, (s + d) % width), device_id_type=MESH)
    for d in range(1, SEATS):
        pl.semaphore_signal(barrier, inc=1, device_id=(near(d), s), device_id_type=MESH)
    for d in range(1, outer):
        pl.semaphore_signal(barrier, inc=1, device_id=(far(d), s), device_id_type=MESH)
    pl.semaphore_signal(barrier, inc=1, device_id=behind, device_id_type=MESH)
    for dx in range(4):
        pl.semaphore_signal(barrier, inc=1, device_id=(twin, chip(dx, 1)), device_id_type=MESH)

    load_z.start()
    gwf[s, 0:KC] = cw[...]
    gwf[s, KC : KC + 1] = cb[...]
    gwf[s, 5:6] = sb[...]
    gwf[s, 6:7] = sg[...]
    gwf[s, 7:8] = jnp.zeros((1, CH), F32)
    gwf[s, 8:WROWS] = dl[...]
    narrow = pwt[...].astype(F32)
    wstage[0:DTR, 0:CH] = sw[...].astype(F32)
    wstage[DTR:CH, 0:CH] = narrow[0:DTR]
    for m in range(3):
        wstage[32 * m : 32 * (m + 1), CH:LANES] = narrow[DTR:, 32 * m : 32 * (m + 1)]
    gwb[s] = wstage[...].astype(BF16)
    tstage[...] = jnp.zeros_like(tstage)
    pl.semaphore_wait(barrier, width + SEATS + outer + 2)

    def place(a, i):
        return (gwf.at[i], gt.at[i], gwb.at[i])[a]

    sent = []
    relayed = [0, 0, 0]

    def relay(a, dx, dy, tx, ty):
        ref = place(a, chip(dx, dy))
        landing = (dx - tx) % 4 * 2 + (dy - ty) % 2
        ssem = s1.at[a, relayed[a]]
        relayed[a] += 1
        frame = twin if ty and a != 1 else f
        sent.append(push(ref, ref, ssem, r1.at[a, landing], (frame, chip(tx, ty))))

    def tail_of(block):
        pair = gt[lax.shift_right_logical(block, 1)].astype(F32)
        odd = jnp.full((TAIL, LANES), block & 1, jnp.int32) == 1
        return jnp.where(odd, pair[TAIL : 2 * TAIL], pair[0:TAIL])

    def share(a, dx, dy):
        ref = place(a, chip(dx, dy))
        k = dx * 2 + dy
        sent.append(push(ref, ref, s2.at[a, k], r2.at[a, k], sibling))

    def take(a, dx, dy):
        ref = place(a, chip(dx, dy))
        remote(ref, ref, s1.at[a, 0], r1.at[a, dx * 2 + dy], sibling).wait_recv()

    def offer(a, targets):
        for tx, ty in targets:
            relay(a, 0, 0, tx, ty)
        share(a, 0, 0)

    def collect(a, items):
        for dx, dy in items:
            take(a, dx, dy)
            share(a, dx, dy)

    def other_side(a):
        take(a, 0, 1)
        relay(a, 0, 1, 1, 0)
        relay(a, 0, 1, 3, 0)
        if a == 1:
            relay(a, 0, 1, 2, 0)
        share(a, 0, 1)

    def neighbours(a):
        for dy in range(2):
            take(a, 1, dy)
            relay(a, 1, dy, 3, 0)
            share(a, 1, dy)
        for dy in range(2):
            take(a, 3, dy)
            share(a, 3, dy)

    def opposite(a):
        for dy in range(2):
            take(a, 2, dy)
            share(a, 2, dy)

    def from_sibling(a):
        for dx in range(4):
            for dy in range(2):
                ref = place(a, chip(dx, dy) - core + 1 - core)
                k = dx * 2 + dy
                remote(ref, ref, s2.at[a, k], r2.at[a, k], sibling).wait_recv()

    offer(0, ((0, 1), (1, 1), (3, 1), (2, 1), (1, 0), (3, 0), (2, 0)))
    load_x.wait()
    for b in range(2):
        ends = xv[BLK * (b + 1) - 16 : BLK * (b + 1)].astype(F32)
        for t in range(KC - 1):
            for j in range(TILES):
                line = ends[13 + t : 14 + t, LANES * j : LANES * (j + 1)]
                at = b * TAIL + t * TILES + j
                tstage[at : at + 1] = line
    gt[s] = tstage[...].astype(BF16)
    offer(1, ((0, 1), (2, 0), (1, 0), (3, 0)))
    offer(2, ((0, 1), (1, 0), (3, 0)))
    listed = [order[j] for j in range(NBF)]

    def inverse(r, carry):
        found = 0
        for j in range(NBF):
            found = jnp.where(listed[j] == r, j, found)
        where_to[r] = found
        return carry

    lax.fori_loop(0, NBF, inverse, 0)
    for b in range(2):
        xf[b, 0:8] = jnp.zeros((8, DI), F32)

    def widen(tile, carry):
        lanes = lanes_of(tile)
        for b in range(2):
            xf[b, 8 : 8 + BLK, lanes] = xv[BLK * b : BLK * (b + 1), lanes].astype(F32)
        return carry

    lax.fori_loop(0, TILES, widen, 0)
    sends[...] = jnp.zeros_like(sends)
    other_side(1)
    other_side(2)
    collect(0, ((3, 0), (1, 0), (0, 1), (3, 1), (1, 1), (2, 0), (2, 1)))
    collect(1, ((1, 0), (3, 0), (2, 0), (1, 1), (3, 1), (2, 1)))
    from_sibling(0)
    for i in range(DI // CH):
        wfa[:, CH * i : CH * (i + 1)] = gwf[i]

    def filtered(b, count, lanes):
        total = wfa[4:5, lanes]
        for k in range(KC):
            total = total + wfa[k : k + 1, lanes] * xf[b, 5 + k : 5 + k + count, lanes]
        return silu(total).astype(BF16)

    def convolve(tile, carry):
        lanes = lanes_of(tile)
        for b in range(2):
            sigt[BLK * b : BLK * (b + 1), lanes] = filtered(b, BLK, lanes)
        return carry

    lax.fori_loop(0, 3, convolve, 0)
    neighbours(2)
    lax.fori_loop(3, 6, convolve, 0)
    from_sibling(1)
    tsel[...] = jnp.zeros_like(tsel)
    tsel[0:TAIL] = tail_of(order[NBF - 1])
    tsend[...] = tsel[...].astype(BF16)
    sent_tail = push(tsend, trecv, st, rt, ahead)
    sent.append(sent_tail)
    opposite(2)
    lax.fori_loop(6, TILES, convolve, 0)
    rate2[...] = -jnp.exp(wfa[8:WROWS]) * LOG2E
    rearranged = scan_rows()
    load_z.wait()

    def gate(chunk, carry):
        lanes = lanes_of(chunk, 256)
        zs = jnp.dot(rearranged, zv[:, lanes], preferred_element_type=F32)
        gz[:, lanes] = silu(zs)
        return carry

    lax.fori_loop(0, DI // 256, gate, 0)
    from_sibling(2)
    for i in range(DI // CH):
        held = gwb[i].astype(F32)
        wba[0:CH, CH * i : CH * (i + 1)] = held[:, 0:CH]
        for m in range(3):
            at = CH * i + 32 * m
            wba[CH:WB, at : at + 32] = held[32 * m : 32 * (m + 1), CH:LANES]
    sent_tail.wait_recv()
    came = trecv[...].astype(F32)[0:TAIL]
    came = jnp.where(jnp.full(came.shape, f, jnp.int32) == 0, 0.0, came)
    for b in range(2):
        at = where_to[2 * s + b]
        found = tail_of(order[jnp.maximum(at - 1, 0)])
        halo = jnp.where(jnp.full(came.shape, at, jnp.int32) == 0, came, found)
        for t in range(KC - 1):
            for j in range(TILES):
                line = halo[t * TILES + j : t * TILES + j + 1]
                xf[b, 5 + t : 6 + t, LANES * j : LANES * (j + 1)] = line

    def heads(tile, carry):
        lanes = lanes_of(tile)
        for b in range(2):
            sigt[BLK * b : BLK * b + 16, lanes] = filtered(b, 16, lanes)
        return carry

    lax.fori_loop(0, TILES, heads, 0)

    def rearrange(chunk, carry):
        lanes = lanes_of(chunk, 256)
        signal[:, lanes] = jnp.dot(rearranged, sigt[:, lanes], preferred_element_type=F32)
        return carry

    lax.fori_loop(0, DI // 256, rearrange, 0)
    proj = lax.dot_general(
        signal[...].astype(BF16),
        wba[DTR:WB].astype(BF16),
        (((1,), (1,)), ((), ())),
        preferred_element_type=F32,
    )
    spread_columns(proj, DTR, in_b)
    rank = proj[:, :DTR]
    high = rank.astype(BF16)
    low = (rank - high.astype(F32)).astype(BF16)

    def steps(chunk, carry):
        lanes = lanes_of(chunk, 256)
        weight = wba[0:DTR, lanes].astype(BF16)
        total = wfa[5:6, lanes] + jnp.dot(low, weight, preferred_element_type=F32)
        total = total + jnp.dot(high, weight, preferred_element_type=F32)
        step[:, lanes] = jnp.maximum(total, 0.0) + jnp.log1p(jnp.exp(-jnp.abs(total)))
        return carry

    lax.fori_loop(0, DI // 256, steps, 0)
    m1 = sub % 4 >= 1
    m2 = sub % 4 >= 2

    def rows_of(t):
        return pl.ds(pl.multiple_of(t * CHUNKS, CHUNKS), CHUNKS)

    def rates_of(lanes):
        return [jnp.broadcast_to(rate2[n : n + 1, lanes], full) for n in range(NS)]

    def block_states(tile, carry):
        lanes = lanes_of(tile)
        rates = rates_of(lanes)

        def one(t, held):
            states, total = held
            rows = rows_of(t)
            now = step[rows, lanes]
            drive = now * signal[rows, lanes]
            states = tuple(
                jnp.exp2(now * rates[n]) * states[n] + in_b[n, rows, :] * drive for n in range(NS)
            )
            return states, total + now

        states, total = lax.fori_loop(0, STEPS, one, ((zero,) * NS, zero), unroll=4)
        sum1 = total + jnp.where(m1, pltpu.roll(total, 1, 0), 0.0)
        sum2 = sum1 + jnp.where(m2, pltpu.roll(sum1, 2, 0), 0.0)
        reach[:, lanes] = jnp.where(m1, pltpu.roll(sum2, 1, 0), 0.0)
        ends = jnp.where(
            sub < 4, jnp.broadcast_to(sum2[3:4], full), jnp.broadcast_to(sum2[7:8], full)
        )
        group = tile // 3
        place = tile % 3
        for h in range(4):
            state_out = zero
            rate_out = zero
            for q in range(4):
                n = 4 * h + q
                decay = jnp.exp2(rates[n] * total)
                one_s = states[n] + jnp.where(m1, decay * pltpu.roll(states[n], 1, 0), 0.0)
                decay2 = jnp.exp2(rates[n] * sum1)
                two_s = one_s + jnp.where(m2, decay2 * pltpu.roll(one_s, 2, 0), 0.0)
                inner[n, :, lanes] = jnp.where(m1, pltpu.roll(two_s, 1, 0), 0.0)
                turn = (q + 5) % 8
                moved = pltpu.roll(two_s, turn, 0) if turn else two_s
                state_out = jnp.where(sub % 4 == q, moved, state_out)
                rate_out = jnp.where(sub % 4 == q, rates[n], rate_out)
            owner = h * 4 + group
            sends[owner, place] = state_out
            sends[owner, 3] = jnp.where(sub % 4 == place, ends, sends[owner, 3])
            rate_own[h, tile] = rate_out
        return carry

    def to_owner(peer):
        return remote(sends.at[peer], recv.at[s], sa.at[peer], ra.at[s], (f, peer))

    def one_group(g, carry):
        lax.fori_loop(g * 3, g * 3 + 3, block_states, 0)
        for h in range(4):
            peer = h * 4 + g

            @pl.when(peer != s)
            def _():
                to_owner(peer).start()

        return carry

    lax.fori_loop(0, 4, one_group, 0)
    recv[s] = sends[s]
    spread_columns(proj, DTR + NS, out_b)

    def own_outputs(tile, carry):
        lanes = lanes_of(tile)
        rates = rates_of(lanes)
        skip = jnp.broadcast_to(wfa[6:7, lanes], full)

        def one(t, held):
            states, total = held
            rows = rows_of(t)
            now = step[rows, lanes]
            sig = signal[rows, lanes]
            drive = now * sig
            total = total + now
            states = tuple(
                jnp.exp2(now * rates[n]) * states[n] + in_b[n, rows, :] * drive for n in range(NS)
            )
            coeffs = [out_b[n, rows, :] for n in range(NS)]
            terms = [coeffs[n] * states[n] for n in range(NS)]
            for n in range(NS):
                grown[n, rows, lanes] = coeffs[n] * jnp.exp2(total * rates[n])
            while len(terms) > 1:
                terms = [a + b for a, b in zip(terms[::2], terms[1::2])]
            y[rows, lanes] = terms[0] + skip * sig
            return states, total

        states = tuple(inner[n, :, lanes] for n in range(NS))
        lax.fori_loop(0, STEPS, one, (states, reach[:, lanes]), unroll=2)
        return carry

    lax.fori_loop(0, 3, own_outputs, 0)
    for d in range(1, width):
        peer = (s + d) % width
        remote(sends.at[peer], recv.at[peer], sa.at[peer], ra.at[peer], (f, peer)).wait_recv()

    def turned(v):
        return pltpu.roll(v, 4, len(v.shape) - 2)

    my_group = s % 4
    my_rates = rate_own[s // 4, pl.ds(my_group * 3, 3)]

    def decays(sums):
        spread = [jnp.broadcast_to(sums[i : i + 1], full) for i in range(3)]
        return jnp.exp2(my_rates * jnp.stack(spread))

    def through(j, carry):
        e, passed = carry
        scan_e[j] = e
        scan_t[j] = passed
        block = order[j]
        got = recv[lax.shift_right_logical(block, 1)]
        odd = jnp.full((4, CHUNKS, LANES), block & 1, jnp.int32) == 1
        got = jnp.where(odd, turned(got), got)
        return decays(got[3]) * e + got[0:3], passed + got[3]

    zero3 = jnp.zeros(slot, F32)
    unit3 = jnp.ones(slot, F32)
    e, passed = lax.fori_loop(0, NBF, through, (zero3, zero), unroll=8)
    p = decays(passed)
    pk1[...] = jnp.where(sub3 < 4, p, turned(e))
    got1[seat] = pk1[...]
    level1 = []
    for d in range(1, SEATS):
        level1.append(push(pk1, got1.at[seat], sb1.at[d], rb1.at[d], (near(d), s)))

    def pack(d, carry):
        i0 = where_to[2 * d]
        i1 = where_to[2 * d + 1]
        bsend[d, 0:3] = jnp.where(sub3 < 4, scan_e[i0], turned(scan_e[i1]))
        bsend[d, 3] = jnp.where(sub < 4, scan_t[i0], turned(scan_t[i1]))
        return carry

    lax.fori_loop(0, width, pack, 0, unroll=4)
    lax.fori_loop(3, 6, own_outputs, 0)
    for copy in sent[: len(sent) // 2]:
        copy.wait_send()
    for copy in level1:
        copy.wait_recv()

    def gather_near(m, carry):
        e_in, p_in, e_all, p_all = carry
        got = got1[m]
        moved = turned(got)
        early = jnp.full(slot, m, jnp.int32) < jnp.full(slot, seat, jnp.int32)
        e_in = jnp.where(early, got * e_in + moved, e_in)
        p_in = jnp.where(early, got * p_in, p_in)
        return e_in, p_in, got * e_all + moved, got * p_all

    begin = (zero3, unit3, zero3, unit3)
    e_in, p_in, e_all, p_all = lax.fori_loop(0, SEATS, gather_near, begin, unroll=SEATS)
    pk2[...] = jnp.where(sub3 < 4, p_all, turned(e_all))
    got2[part] = pk2[...]
    level2 = []
    for d in range(1, outer):
        level2.append(push(pk2, got2.at[part], sc.at[d], rc.at[d], (far(d), s)))
    back[s] = bsend[s]
    returns = []
    for d in range(1, width):
        peer = (s + d) % width
        returns.append(push(bsend.at[peer], back.at[s], sd.at[peer], rd.at[s], (f, peer)))
    lax.fori_loop(6, 9, own_outputs, 0)
    for copy in sent[len(sent) // 2 :] + level1:
        copy.wait_send()
    for copy in level2:
        copy.wait_recv()

    def gather_far(m, start):
        got = got2[m]
        early = jnp.full(slot, m, jnp.int32) < jnp.full(slot, part, jnp.int32)
        return jnp.where(early, got * start + turned(got), start)

    start = lax.fori_loop(0, outer, gather_far, zero3, unroll=4)
    start = p_in * start + e_in

    first = jnp.where(sub < 4, start[0], turned(start[1]))
    fsend[...] = jnp.concatenate([first, start[2]], axis=0).astype(BF16)
    fback[s] = fsend[...]
    starts = []
    for d in range(1, width):
        peer = (s + d) % width
        starts.append(push(fsend, fback.at[s], sf.at[peer], rf.at[s], (f, peer)))
    lax.fori_loop(9, 12, own_outputs, 0)
    for copy in level2 + returns:
        copy.wait_send()
    for d in range(1, width):
        to_owner((s + d) % width).wait_send()
    for d in range(1, width):
        peer = (s + d) % width
        remote(bsend.at[peer], back.at[peer], sd.at[peer], rd.at[peer], (f, peer)).wait_recv()

    def both(tile8, r):
        return jnp.where(
            sub < 4,
            jnp.broadcast_to(tile8[r : r + 1], full),
            jnp.broadcast_to(tile8[4 + r : 5 + r], full),
        )

    def complete(g, place):
        lanes = lanes_of(g * 3 + place)
        rates = rates_of(lanes)
        passed = both(back[g, 3], place)
        entering = []
        for h in range(4):
            came = back[h * 4 + g, place]
            begun = fback[h * 4 + g].astype(F32)
            for q in range(4):
                r = place * 4 + q
                line = jnp.broadcast_to(begun[r : r + 1], full)
                entering.append(both(came, q) + jnp.exp2(rates[4 * h + q] * passed) * line)

        def one(t, carry):
            rows = rows_of(t)
            terms = [grown[n, rows, lanes] * entering[n] for n in range(NS)]
            while len(terms) > 1:
                terms = [a + b for a, b in zip(terms[::2], terms[1::2])]
            scanned = (y[rows, lanes] + terms[0]).astype(BF16).astype(F32)
            y[rows, lanes] = scanned * gz[rows, lanes]
            return carry

        lax.fori_loop(0, STEPS, one, 0, unroll=4)
        gated[:, lanes] = y[:, lanes].astype(BF16)

    undo = token_rows()

    def one_group_back(g, carry):
        for h in range(4):
            peer = h * 4 + g

            @pl.when(peer != s)
            def _():
                remote(fsend, fback.at[peer], sf.at[peer], rf.at[peer], (f, peer)).wait_recv()

        for place in range(3):
            complete(g, place)
        lanes = lanes_of(g, 3 * LANES)
        out[:, lanes] = jnp.dot(undo, gated[:, lanes], preferred_element_type=F32).astype(BF16)
        return carry

    lax.fori_loop(0, 4, one_group_back, 0)
    for copy in starts:
        copy.wait_send()


def shards(
    inner_x,
    inner_z,
    conv_weight,
    conv_bias,
    proj_weight,
    step_weight,
    step_bias,
    decay_log,
    skip_gain,
    out_weight,
    order_table,
):
    frames, rows, columns, channels = inner_x.shape
    space = lax.axis_size("space")
    outer = lax.axis_size("tm") // SEATS
    dma = pltpu.SemaphoreType.DMA
    slot = (3, CHUNKS, LANES)
    anyw = pl.BlockSpec(memory_space=pl.ANY)
    vm = pl.BlockSpec(memory_space=pltpu.VMEM)
    held = [
        ((TOK, DI), BF16),
        ((TOK, DI), BF16),
        ((space, WROWS, CH), F32),
        ((space, CH, LANES), BF16),
        ((space, PAIR, LANES), BF16),
        ((PAIR, LANES), F32),
        ((CH, LANES), F32),
        ((TROWS, LANES), F32),
        ((TROWS, LANES), BF16),
        ((TROWS, LANES), BF16),
        None,
        ((WROWS, DI), F32),
        ((WB, DI), F32),
        ((2, BLK + 8, DI), F32),
        ((TOK, DI), BF16),
        ((TOK, DI), F32),
        ((TOK, DI), F32),
        ((TOK, DI), F32),
        ((NS, DI), F32),
        ((4, TILES, CHUNKS, LANES), F32),
        ((NS, TOK, LANES), F32),
        ((NS, TOK, LANES), F32),
        ((NS, CHUNKS, DI), F32),
        ((CHUNKS, DI), F32),
        ((TOK, DI), F32),
        ((TOK, DI), BF16),
        ((NS, TOK, DI), F32),
        ((space, 4, CHUNKS, LANES), F32),
        ((space, 4, CHUNKS, LANES), F32),
        ((NBF,) + slot, F32),
        ((NBF, CHUNKS, LANES), F32),
        (slot, F32),
        ((SEATS,) + slot, F32),
        (slot, F32),
        ((outer,) + slot, F32),
        ((space, 4, CHUNKS, LANES), F32),
        ((space, 4, CHUNKS, LANES), F32),
        ((16, LANES), BF16),
        ((space, 16, LANES), BF16),
    ]
    scratch = [pltpu.SMEM((NBF,), jnp.int32) if h is None else pltpu.VMEM(*h) for h in held]
    scratch += [dma((2,))] + [dma((3, 8))] * 4 + [dma] * 2
    scratch += [dma((16,))] * 2 + [dma((8,))] * 4 + [dma((16,))] * 4
    gated = pl.pallas_call(
        layer,
        out_shape=jax.ShapeDtypeStruct((TOK, DI), BF16),
        in_specs=[anyw, anyw] + [vm] * 7 + [pl.BlockSpec(memory_space=pltpu.SMEM)],
        out_specs=vm,
        scratch_shapes=scratch,
        compiler_params=pltpu.CompilerParams(
            collective_id=0, has_side_effects=True, vmem_limit_bytes=VMEM_LIMIT
        ),
        name="layer",
    )(
        inner_x.reshape(TOK, DI),
        inner_z.reshape(TOK, DI),
        conv_weight,
        conv_bias.reshape(1, CH),
        proj_weight.T,
        step_weight,
        step_bias.reshape(1, CH),
        decay_log,
        skip_gain.reshape(1, CH),
        order_table,
    )
    mixed = jnp.dot(gated, out_weight, preferred_element_type=F32).astype(BF16)
    return mixed.reshape(frames, rows, columns, D)


def solution(mesh):
    in_specs = (
        P("tm", "space", None, None),
        P("tm", "space", None, None),
        P(None, "space"),
        P("space"),
        P("space", None),
        P(None, "space"),
        P("space"),
        P(None, "space"),
        P("space"),
        P(),
        P(),
    )
    out_specs = P("tm", "space", None, None)
    return jax.shard_map(shards, mesh=mesh, in_specs=in_specs, out_specs=out_specs, check_vma=False)
```
